256 devices in a mesh: hist: 32 (over x, z), head: 8 (over y, core).
Axes of the slice: x: 4, y: 4, z: 8, core: 2. Of those that a mesh axis runs over, the one named last changes fastest.
Arguments:
- queries: bfloat16 [3584, 5120], P('hist', 'head'), as said below
- cache_keys: bfloat16 [43008, 5120], P('hist', 'head'), as said below
- cache_values: bfloat16 [43008, 5120], P('hist', 'head'), may hold values from -6 to 6
- hist_lengths: int32 [32], P('hist'), may hold values from 336 to 1344, as said below
- frame_bounds: int32 [4], replicated, may hold values from 21504 to 43008, as said below
- latent: bfloat16 [384, 3, 96, 160], P('head', None, 'hist'), as said below
- norm_gain: float32 [384], P('head'), may hold values from 0.1 to 1.9
- conv_weight: bfloat16 [3, 3, 3, 384, 384], P(None, None, None, 'head'), may hold values from -0.0625 to 0.0625
- conv_bias: float32 [384], P('head'), may hold values from -3 to 3
Outputs:
- attention: bfloat16 [3584, 5120], P('hist', 'head')
- vae_out: bfloat16 [384, 96, 160], P('head', 'hist')
The draws below stay inside these ranges and needn't reach their ends.
Inputs may be any that keep to these rules, and one draw needn't show every extreme that they name: `queries`: Real-valued query vectors. `cache_keys`: Real-valued key vectors. `hist_lengths`: some block is full and some block holds exactly 336 filled slots. `frame_bounds`: never falling from one span to the next; the last span sees all 43008 slots. `latent`: Real-valued features.
All inputs are finite; a program needn't handle non-finite values.
Results may differ from the reference program's by a relative error of at most 0.017.
Values may be sent and summed in bfloat16 or wider, within the bound.
No kernel may reach another device: no remote copies, remote signals or barrier semaphores. Data moves between devices by JAX's collectives and lax.ppermute only.
A program may use at most 128 MiB of HBM per device.

```python
import math
import jax
import jax.numpy as jnp
from jax import lax

HEAD_DIM = 128
HEADS = 40
CHANNELS = 384
QUERIES = 3584
HIST_DEV = 1344
HISTORY = 43008
SHARDS = 32
FRAMES = 4
ROWS = 96
WIDTH = 160
N_HIST = 32


def draw_queries(key, part):
    key = jax.random.fold_in(key, 11)
    base_key, scale_key = jax.random.split(key)
    row_scale = jnp.exp(jax.random.uniform(scale_key, (QUERIES, 1), jnp.float32, math.log(0.8), math.log(8.0)))
    values = jax.random.normal(base_key, (QUERIES, HEADS * HEAD_DIM), jnp.float32) * row_scale
    return values.astype(jnp.bfloat16)


def draw_cache_keys(key, part):
    key = jax.random.fold_in(key, 21)
    base_key, scale_key = jax.random.split(key)
    row_scale = jnp.exp(jax.random.uniform(scale_key, (HISTORY, 1), jnp.float32, math.log(0.6), math.log(1.7)))
    values = jax.random.normal(base_key, (HISTORY, HEADS * HEAD_DIM), jnp.float32) * row_scale
    return values.astype(jnp.bfloat16)


def draw_hist_lengths(key, part):
    key = jax.random.fold_in(key, 31)
    first_key, second_key = jax.random.split(key)
    filled = jax.random.randint(first_key, (SHARDS,), HIST_DEV // 4, HIST_DEV + 1, jnp.int32)
    order = jax.random.permutation(second_key, SHARDS)
    filled = filled.at[order[0]].set(HIST_DEV)
    filled = filled.at[order[1]].set(HIST_DEV // 4)
    return filled.astype(jnp.int32)


def draw_frame_bounds(key, part):
    key = jax.random.fold_in(key, 41)
    bounds = jnp.sort(jax.random.randint(key, (FRAMES,), HISTORY // 2, HISTORY + 1, jnp.int32))
    bounds = bounds.at[0].set(HISTORY // 2)
    bounds = bounds.at[FRAMES - 1].set(HISTORY)
    return bounds.astype(jnp.int32)


def draw_latent(key, part):
    key = jax.random.fold_in(key, 51)
    grade = jnp.arange(CHANNELS, dtype=jnp.float32) / (CHANNELS - 1)
    rise = jnp.exp(math.log(3.0) * grade)[:, None, None, None]
    values = jax.random.normal(key, (CHANNELS, 3, ROWS, WIDTH), jnp.float32) * rise
    return values.astype(jnp.bfloat16)


def level_of(key, extent, shards, least, largest):
    factor_of, own = 1.0, jax.random.fold_in(key, 6)
    for axis_at, parts in shards:
        draws = jnp.exp(jax.random.uniform(jax.random.fold_in(own, axis_at), (parts,), jnp.float32, least / len(shards), largest / len(shards)))
        factor_of = factor_of * jnp.repeat(draws, extent[axis_at] // parts).reshape([-1 if axis == axis_at else 1 for axis in range(len(extent))])
    return factor_of


def normal_values(stream_key, extent, deviation, reach, cuts=(), held_as=jnp.bfloat16):
    entries = jax.random.normal(stream_key, extent, jnp.float32) * deviation
    if len(cuts) > 0:
        entries = level_of(stream_key, extent, cuts, -0.22, 0.18) * entries
    return jnp.clip(entries, min=-reach, max=reach).astype(held_as)


def setup_inputs(seed: int = 0) -> dict:
    seeds = jax.random.split(jax.random.key(seed), 10)
    return {
        "queries": draw_queries(jax.random.fold_in(seeds[9], 71), 0),
        "cache_keys": draw_cache_keys(jax.random.fold_in(seeds[9], 71), 0),
        "cache_values": normal_values(seeds[2], (HISTORY, HEADS * HEAD_DIM), 1.0, 6.0, ((0, 32), (1, 8))),
        "hist_lengths": draw_hist_lengths(jax.random.fold_in(seeds[9], 71), 0),
        "frame_bounds": draw_frame_bounds(jax.random.fold_in(seeds[9], 71), 0),
        "latent": draw_latent(jax.random.fold_in(seeds[9], 71), 0),
        "norm_gain": jnp.clip(1.0 + 0.18 * jax.random.normal(seeds[6], (CHANNELS,), jnp.float32), 0.1, 1.9),
        "conv_weight": normal_values(seeds[7], (3, 3, 3, CHANNELS, CHANNELS), (27 * CHANNELS) ** -0.5, 0.0625, ((3, 8),)),
        "conv_bias": normal_values(seeds[8], (CHANNELS,), 0.5, 3.0, ((0, 8),), jnp.float32),
    }


mask_fill = -1e+30
norm_eps = 1e-06

def head_attention(query_head, key_head, value_head, row_bound, hist_lengths):
    score_scale = HEAD_DIM ** (-0.5)

    def one_block(block):
        first = (block * HIST_DEV).astype(jnp.int32)
        key_part = lax.dynamic_slice_in_dim(key_head, first, HIST_DEV, 0)
        value_part = lax.dynamic_slice_in_dim(value_head, first, HIST_DEV, 0)
        scores = jnp.dot(query_head, key_part.T, preferred_element_type=jnp.float32) * score_scale
        places = jnp.arange(HIST_DEV, dtype=jnp.int32)
        visible = (places < hist_lengths[block])[None, :] & ((first + places)[None, :] < row_bound[:, None])
        scores = jnp.where(visible, scores, mask_fill)
        highest = lax.optimization_barrier(jnp.max(scores, axis=1))
        weights = jnp.exp(scores - highest[:, None]).astype(jnp.bfloat16)
        weights = lax.optimization_barrier(weights).astype(jnp.float32)
        totals = lax.optimization_barrier(jnp.sum(weights, axis=1))
        weighted = jnp.dot(weights, value_part, preferred_element_type=jnp.float32)
        return (highest, totals, weighted)
    highest, totals, weighted = lax.map(one_block, jnp.arange(N_HIST, dtype=jnp.int32))
    common = lax.optimization_barrier(jnp.max(highest, axis=0))
    factor = jnp.exp(highest - common[None, :])
    numerator = lax.optimization_barrier(jnp.sum(weighted * factor[:, :, None], axis=0))
    denominator = lax.optimization_barrier(jnp.sum(totals * factor, axis=0))
    return numerator / denominator[:, None]

def reference(queries, cache_keys, cache_values, hist_lengths, frame_bounds, latent, norm_gain, conv_weight, conv_bias):
    frame_of = jnp.arange(QUERIES, dtype=jnp.int32) * FRAMES // QUERIES
    row_bound = frame_bounds[frame_of]
    query_heads = jnp.transpose(queries.astype(jnp.float32).reshape(QUERIES, HEADS, HEAD_DIM), (1, 0, 2))
    key_heads = jnp.transpose(cache_keys.astype(jnp.float32).reshape(HISTORY, HEADS, HEAD_DIM), (1, 0, 2))
    value_heads = jnp.transpose(cache_values.astype(jnp.float32).reshape(HISTORY, HEADS, HEAD_DIM), (1, 0, 2))

    def per_head(operands):
        return head_attention(operands[0], operands[1], operands[2], row_bound, hist_lengths)
    result = lax.map(per_head, (query_heads, key_heads, value_heads))
    attention = jnp.transpose(result, (1, 0, 2)).reshape(QUERIES, HEADS * HEAD_DIM).astype(jnp.bfloat16)
    features = latent.astype(jnp.float32)
    mean_sq = lax.optimization_barrier(jnp.sum(features * features, axis=0)) / CHANNELS
    scaled = features * lax.rsqrt(mean_sq + norm_eps)[None] * norm_gain.astype(jnp.float32)[:, None, None, None]
    activated = jax.nn.silu(scaled).astype(jnp.bfloat16)
    activated = lax.optimization_barrier(activated).astype(jnp.float32)
    padded = jnp.pad(activated, ((0, 0), (0, 0), (1, 1), (1, 1)))
    summed = jnp.zeros((CHANNELS, ROWS, WIDTH), jnp.float32)
    for tap_time in range(3):
        for tap_row in range(3):
            for tap_col in range(3):
                window = padded[:, tap_time, tap_row:tap_row + ROWS, tap_col:tap_col + WIDTH]
                kernel = conv_weight[tap_time, tap_row, tap_col].astype(jnp.float32)
                summed = summed + jnp.einsum('cyx,co->oyx', window, kernel)
    vae_out = (summed + conv_bias.astype(jnp.float32)[:, None, None]).astype(jnp.bfloat16)
    return (attention, vae_out)
```

```python
import functools
import math

import jax
import jax.numpy as jnp
from jax import lax
from jax.experimental import pallas as pl
from jax.experimental.pallas import tpu as pltpu
from jax.sharding import PartitionSpec as P

HEAD_DIM = 128
CHANNELS = 384
FRAMES = 4
NX = 4
NZ = 8
NY = 4

NEG = -1e30
LOG2E = math.log2(math.e)
norm_eps = 1e-06
VMEM = 56 << 20


def hist_shift(dx, dz):
    return [
        (x * NZ + z, ((x + dx) % NX) * NZ + (z + dz) % NZ) for x in range(NX) for z in range(NZ)
    ]


def head_shift(dy, flip):
    return [
        (y * 2 + c, ((y + dy) % NY) * 2 + (c ^ flip)) for y in range(NY) for c in range(2)
    ]


def dot(a, b, dims):
    return lax.dot_general(a, b, (dims, ((), ())), preferred_element_type=jnp.float32)


def pack_queries_kernel(q_ref, *outs):
    x = lax.axis_index("hist") // NZ
    for d, out in enumerate(outs):
        head = lax.rem(x + d, NX)
        out[:, :128] = q_ref[:, pl.ds(pl.multiple_of(head * 128, 128), 128)]
        out[:, 128:] = q_ref[:, 512:640]


def pack_queries(queries):
    rows = queries.shape[0]
    return pl.pallas_call(
        pack_queries_kernel,
        out_shape=[jax.ShapeDtypeStruct((rows, 256), jnp.bfloat16)] * NX,
        name="pack_q",
    )(queries)


def pack_cache_kernel(len_ref, k_ref, v_ref, *outs):
    x = lax.axis_index("hist") // NZ
    rows = k_ref.shape[0]
    length = len_ref[0]
    row = lax.broadcasted_iota(jnp.int32, (16, 256), 0)
    tail = jnp.where(row == 0, length // 64, jnp.where(row == 1, lax.rem(length, 64), 0))
    for d, out in enumerate(outs):
        head = lax.rem(x + d, NX)
        out[:rows, :128] = k_ref[:, pl.ds(pl.multiple_of(head * 128, 128), 128)]
        out[:rows, 128:] = v_ref[:, pl.ds(pl.multiple_of(head * 128, 128), 128)]
        out[rows:, :] = tail.astype(jnp.float32).astype(jnp.bfloat16)


def pack_cache(lengths, keys, values):
    rows = keys.shape[0]
    vmem = pl.BlockSpec(memory_space=pltpu.VMEM)
    return pl.pallas_call(
        pack_cache_kernel,
        in_specs=[pl.BlockSpec(memory_space=pltpu.SMEM), vmem, vmem],
        out_shape=[jax.ShapeDtypeStruct((rows + 16, 256), jnp.bfloat16)] * NX,
        compiler_params=pltpu.CompilerParams(vmem_limit_bytes=VMEM),
        name="pack_kv",
    )(lengths, keys, values)


def limits_of(length, block_x, x, z, rows, bounds_ref):
    out = []
    for slot in range(NX):
        frame = lax.rem(x - slot + NX, NX)
        seen = jnp.minimum(length, bounds_ref[frame] - (block_x * NZ + z) * rows)
        out.append(jnp.clip(seen, 0, rows))
    return out


def unit(q_of, n, group, k_of, v_of, limits, rows, acc_ref, l_ref, m_ref, c2):
    part = group // NX
    longest = functools.reduce(jnp.maximum, limits)

    def step(count):
        row = lax.broadcasted_iota(jnp.int32, (group, 1), 0)
        limit = jnp.full((group, 1), limits[0], jnp.int32)
        for slot in range(1, NX):
            limit = jnp.where(row >= slot * part, limits[slot], limit)
        lane = lax.broadcasted_iota(jnp.int32, (1, count), 1)
        k = k_of(count)
        v = jnp.concatenate([v_of(count), jnp.ones((count, 128), jnp.bfloat16)], axis=1)

        def scores(g):
            return jnp.where(lane < limit, dot(q_of(g), k, ((1,), (1,))), NEG)

        s = scores(0)
        for g in range(n):
            later = scores(g + 1) if g + 1 < n else None
            here = slice(g * group, (g + 1) * group)
            old = m_ref[here, :]
            new = jnp.maximum(old, jnp.max(s, axis=1, keepdims=True) * c2)
            p = jnp.exp2(s * c2 - new[:, :1]).astype(jnp.bfloat16)
            r = dot(p, v, ((1,), (0,)))
            a = jnp.exp2(old - new)
            acc_ref[here, :] = acc_ref[here, :] * a + r[:, :128]
            l_ref[here, :] = l_ref[here, :] * a + r[:, 128:]
            m_ref[here, :] = new
            s = later

    low = 0
    for size in (512, 896, rows):
        pl.when((longest > low) & (longest <= size))(functools.partial(step, size))
        low = size


def own_kernel(n, rows, c2, len_ref, bounds_ref, kv, k4, v4, *refs):
    q_refs, outs = refs[:n], refs[n : 2 * n]
    acc_ref, l_ref, m_ref = refs[2 * n :]
    h = lax.axis_index("hist")
    x, z = h // NZ, lax.rem(h, NZ)
    group = q_refs[0].shape[0]
    limits = limits_of(len_ref[0], x, x, z, rows, bounds_ref)
    heads = [
        (lambda c: kv[:c, :128], lambda c: kv[:c, 128:]),
        (lambda c: k4[:c, :], lambda c: v4[:c, :]),
    ]
    for head, (k_of, v_of) in enumerate(heads):
        acc_ref[...] = jnp.zeros_like(acc_ref)
        l_ref[...] = jnp.ones_like(l_ref)
        m_ref[...] = jnp.full_like(m_ref, NEG)
        unit(
            lambda g, at=head * 128: q_refs[g][:, at : at + 128],
            n, group, k_of, v_of, limits, rows, acc_ref, l_ref, m_ref, c2,
        )
        l = l_ref[...]
        log = m_ref[...] + jnp.log2(l)
        normed = acc_ref[...] / l
        for g, out in enumerate(outs):
            here = slice(g * group, (g + 1) * group)
            out[:, head * 128 : (head + 1) * 128] = normed[here, :]
            out[:, 256 + head * 128 : 384 + head * 128] = log[here, :]


def cost(n, group, rows, units):
    work = n * group * rows * units
    return pl.CostEstimate(flops=1200 * work, bytes_accessed=units * rows * 512, transcendentals=work)


def attn_own(length, bounds, kv, keys, values, groups, c2):
    rows = keys.shape[0]
    n, group = len(groups), groups[0].shape[0]
    smem = pl.BlockSpec(memory_space=pltpu.SMEM)
    full = lambda a: pl.BlockSpec(a.shape, lambda i: (0, 0))
    last = pl.BlockSpec((rows, 128), lambda i: (0, NX))
    return pl.pallas_call(
        functools.partial(own_kernel, n, rows, c2),
        grid=(1,),
        out_shape=[jax.ShapeDtypeStruct((group, 512), jnp.float32)] * n,
        in_specs=[smem, smem, full(kv), last, last] + [full(a) for a in groups],
        out_specs=[pl.BlockSpec((group, 512), lambda i: (0, 0))] * n,
        scratch_shapes=[pltpu.VMEM((n * group, 128), jnp.float32)] * 3,
        compiler_params=pltpu.CompilerParams(vmem_limit_bytes=VMEM),
        cost_estimate=cost(n, group, rows, 2),
        name="attn_own",
    )(length, bounds, kv, keys, values, *groups)


def far_kernel(n, halves, rows, c2, bounds_ref, *refs):
    kvs = refs[: NX - 1]
    refs = refs[NX - 1 :]
    q_refs, starts, outs = refs[:n], refs[n : 2 * n], refs[2 * n : 3 * n + halves]
    buf, acc_ref, l_ref, m_ref, sems = refs[3 * n + halves :]
    copies = [pltpu.make_async_copy(kv, buf.at[u], sems.at[u]) for u, kv in enumerate(kvs)]
    for c in copies:
        c.start()
    h = lax.axis_index("hist")
    x, z = h // NZ, lax.rem(h, NZ)
    group = q_refs[0].shape[0]
    l_ref[...] = jnp.ones_like(l_ref)
    for g, start in enumerate(starts):
        here = slice(g * group, (g + 1) * group)
        acc_ref[here, :] = start[:, :128]
        m_ref[here, :] = start[:, 256:384]
    for c in copies:
        c.wait()

    def body(u, carry):
        tail = buf[u, rows : rows + 16, :128].astype(jnp.float32)
        row = lax.broadcasted_iota(jnp.int32, (16, 128), 0)
        high = jnp.max(jnp.where(row == 0, tail, 0.0))
        low = jnp.max(jnp.where(row == 1, tail, 0.0))
        length = (high * 64.0 + low).astype(jnp.int32)
        limits = limits_of(length, lax.rem(x - u - 1 + NX, NX), x, z, rows, bounds_ref)
        unit(
            lambda g: q_refs[g][:, :128],
            n, group, lambda c: buf[u, :c, :128], lambda c: buf[u, :c, 128:],
            limits, rows, acc_ref, l_ref, m_ref, c2,
        )
        return carry

    lax.fori_loop(0, NX - 1, body, 0)
    l = l_ref[...]
    log = m_ref[...] + jnp.log2(l)
    normed = (acc_ref[...] / l).astype(jnp.bfloat16)
    at = 0
    for g in range(n):
        cut = 2 if g == 0 and halves else 1
        size = group // cut
        for k in range(cut):
            there = slice(k * size, (k + 1) * size)
            here = slice(g * group + k * size, g * group + (k + 1) * size)
            out = outs[at]
            at += 1
            out[:size, :128] = normed[here, :]
            out[:size, 128:] = starts[g][there, 128:256].astype(jnp.bfloat16)
            write_logs(out, size, [log[here, :], starts[g][there, 384:]])


def stat_rows(rows):
    return 16 * (-(-rows // 256))


def attn_far(bounds, kvs, groups, starts, halves, c2):
    rows = kvs[0].shape[0] - 16
    n, group = len(groups), groups[0].shape[0]
    smem = pl.BlockSpec(memory_space=pltpu.SMEM)
    vmem = pl.BlockSpec(memory_space=pltpu.VMEM)
    anys = pl.BlockSpec(memory_space=pl.ANY)
    sizes = [group // 2] * (2 * halves) + [group] * (n - halves)
    return pl.pallas_call(
        functools.partial(far_kernel, n, halves, rows, c2),
        out_shape=[jax.ShapeDtypeStruct((s + stat_rows(s), 256), jnp.bfloat16) for s in sizes],
        in_specs=[smem] + [anys] * (NX - 1) + [vmem] * (2 * n),
        out_specs=[vmem] * len(sizes),
        scratch_shapes=[pltpu.VMEM((NX - 1, rows + 16, 256), jnp.bfloat16)]
        + [pltpu.VMEM((n * group, 128), jnp.float32)] * 3
        + [pltpu.SemaphoreType.DMA((NX - 1,))],
        compiler_params=pltpu.CompilerParams(vmem_limit_bytes=VMEM),
        cost_estimate=cost(n, group, rows, NX - 1),
        name="attn_far",
    )(bounds, *kvs, *groups, *starts)


def three_parts(value):
    high = value.astype(jnp.bfloat16).astype(jnp.float32)
    rest = value - high
    mid = rest.astype(jnp.bfloat16).astype(jnp.float32)
    return [high, mid, rest - mid]


def write_logs(out, rows, logs):
    lanes = -(-rows // 128) * 128
    lane = lax.broadcasted_iota(jnp.int32, (rows, 128), 1)
    table = jnp.zeros((rows, 128), jnp.float32)
    for head, lg in enumerate(logs):
        for k, piece in enumerate(three_parts(lg)):
            table = jnp.where(lane == k * len(logs) + head, piece, table)
    if lanes > rows:
        table = jnp.concatenate([table, jnp.zeros((lanes - rows, 128), jnp.float32)], axis=0)
    flat = table.T[:16, :].astype(jnp.bfloat16)
    for k in range(-(-lanes // 256)):
        wide = min(256, lanes - k * 256)
        at = rows + 16 * k
        out[at : at + 16, :wide] = flat[:, k * 256 : k * 256 + wide]
        if wide < 256:
            out[at : at + 16, wide:] = jnp.zeros((16, 256 - wide), jnp.bfloat16)


def read_logs(ref, rows, heads):
    lanes = -(-rows // 128) * 128
    pieces = [
        ref[rows + 16 * k : rows + 16 * (k + 1), : min(256, lanes - 256 * k)].astype(jnp.float32)
        for k in range(-(-lanes // 256))
    ]
    flat = pieces[0] if len(pieces) == 1 else jnp.concatenate(pieces, axis=1)
    return [
        flat[h : h + 1, :] + flat[heads + h : heads + h + 1, :] + flat[2 * heads + h : 2 * heads + h + 1, :]
        for h in range(heads)
    ]


def weights_of(rows_list):
    top = functools.reduce(jnp.maximum, rows_list)
    raw = [jnp.exp2(r - top) for r in rows_list]
    total = functools.reduce(jnp.add, raw)
    return [r / total for r in raw], top + jnp.log2(total)


def columns_of(rows_list):
    lanes = rows_list[0].shape[1]
    table = jnp.concatenate(
        rows_list + [jnp.zeros((128 - len(rows_list), lanes), jnp.float32)], axis=0
    )
    return table.T


def join(logs, datas):
    top = functools.reduce(jnp.maximum, logs)
    raw = [jnp.exp2(lg - top) for lg in logs]
    total = functools.reduce(jnp.add, raw)
    out = functools.reduce(
        jnp.add, [d.astype(jnp.float32) * (r / total) for r, d in zip(raw, datas)]
    )
    return out, top + jnp.log2(total)


def relay_kernel(rows, *refs):
    half = rows // 2
    for k in range(2):
        mine, next_, part, out = (refs[i * 2 + k] for i in range(4))
        tables = [columns_of(read_logs(r, rows, 2)) for r in (mine, next_)]
        small = columns_of(read_logs(part, half, 2))
        joint = []
        for head in range(2):
            cols = slice(head * 128, (head + 1) * 128)
            logs = [t[:rows, head : head + 1] for t in tables]
            datas = [r[:rows, cols].astype(jnp.float32) for r in (mine, next_)]
            fill = jnp.full((half, 1), NEG, jnp.float32)
            zero = jnp.zeros((half, 128), jnp.float32)
            log = [small[:half, head : head + 1], fill]
            data = [part[:half, cols].astype(jnp.float32), zero]
            if k == 1:
                log, data = log[::-1], data[::-1]
            logs.append(jnp.concatenate(log, axis=0))
            datas.append(jnp.concatenate(data, axis=0))
            total, lg = join(logs, datas)
            out[:rows, cols] = total.astype(jnp.bfloat16)
            joint.append(jnp.broadcast_to(lg, (rows, 128)))
        write_logs(out, rows, joint)


def relay(mine, nexts, parts, rows):
    return pl.pallas_call(
        functools.partial(relay_kernel, rows),
        out_shape=[jax.ShapeDtypeStruct((rows + stat_rows(rows), 256), jnp.bfloat16)] * 2,
        compiler_params=pltpu.CompilerParams(vmem_limit_bytes=VMEM),
        cost_estimate=pl.CostEstimate(flops=4 * 10**9, bytes_accessed=1 << 20, transcendentals=0),
        name="relay",
    )(*mine, *nexts, *parts)


def merge_kernel(rows, part, n, *refs):
    ins, outs = refs[:n], refs[n:]
    logs = [read_logs(r, rows, 2) for r in ins]
    w0, _ = weights_of([lg[0] for lg in logs])
    w1, joint = weights_of([lg[1] for lg in logs])
    table = columns_of(w0 + w1 + [joint])
    sums = []
    for head in range(2):
        total = jnp.zeros((rows, 128), jnp.float32)
        for k, r in enumerate(ins):
            at = head * n + k
            total += table[:rows, at : at + 1] * r[:rows, head * 128 : (head + 1) * 128].astype(
                jnp.float32
            )
        sums.append(total.astype(jnp.bfloat16))
    joint_col = jnp.broadcast_to(table[:rows, 2 * n : 2 * n + 1], (rows, 128))
    for d, out in enumerate(outs):
        here = slice(d * part, (d + 1) * part)
        out[:part, :128] = sums[0][here, :]
        out[:part, 128:] = sums[1][here, :]
        write_logs(out, part, [joint_col[here, :]])


def merge(payloads, part):
    rows = part * NX
    return pl.pallas_call(
        functools.partial(merge_kernel, rows, part, len(payloads)),
        out_shape=[jax.ShapeDtypeStruct((part + 16, 256), jnp.bfloat16)] * NX,
        compiler_params=pltpu.CompilerParams(vmem_limit_bytes=VMEM),
        cost_estimate=pl.CostEstimate(flops=4 * 10**9, bytes_accessed=1 << 20, transcendentals=0),
        name="merge",
    )(*payloads)


def finish_kernel(part, *refs):
    ins, out = refs[:NX], refs[NX]
    x = lax.axis_index("hist") // NZ
    w, _ = weights_of([read_logs(r, part, 1)[0] for r in ins])
    table = columns_of(w)
    total = jnp.zeros((part, 128), jnp.float32)
    for d, r in enumerate(ins):
        head = lax.rem(x + d, NX)
        out[:, pl.ds(pl.multiple_of(head * 128, 128), 128)] = r[:part, :128]
        total += table[:part, d : d + 1] * r[:part, 128:].astype(jnp.float32)
    out[:, 512:640] = total.astype(jnp.bfloat16)


def finish(parts, part):
    return pl.pallas_call(
        functools.partial(finish_kernel, part),
        out_shape=jax.ShapeDtypeStruct((part, (NX + 1) * 128), jnp.bfloat16),
        name="finish",
    )(*parts)


def along_x(value, d):
    return lax.ppermute(value, "hist", hist_shift(d, 0))


def along_z(value, d):
    return lax.ppermute(value, "hist", hist_shift(0, d))


def attention_part(queries, keys, values, length, bounds):
    part = queries.shape[0]
    rows = part * NX
    half = rows // 2
    c2 = HEAD_DIM ** (-0.5) * LOG2E
    packed = pack_queries(queries)
    mine = [packed[0]] + [along_x(packed[d], d) for d in range(1, NX)]
    keys, values, _ = lax.optimization_barrier((keys, values, packed[0]))
    cache = pack_cache(length, keys, values)
    kvs = [along_x(cache[d], d) for d in range(1, NX)]

    G = {0: jnp.concatenate(mine, axis=0)}
    for e in (1, -1, 2, -2):
        G[e] = along_z(G[0], e)
    G[3] = along_z(G[2], 1)
    G[-3] = along_z(G[-2], -1)
    G[4] = jnp.concatenate([along_z(G[2][:half], 2), along_z(G[-2][half:], -2)], axis=0)

    S = {}
    for turn in ((0,), (1, -1), (2, -2), (3, -3, 4)):
        done = attn_own(length, bounds, cache[0], keys, values, [G[e] for e in turn], c2)
        S.update(zip(turn, done))

    def far(turn, halves=0):
        return attn_far(bounds, kvs, [G[e] for e in turn], [S[e] for e in turn], halves, c2)

    low, high, plus3, minus3 = far((4, 3, -3), 1)
    nexts = [along_z(plus3, -1), along_z(minus3, 1)]
    parts = [along_z(low, -2), along_z(high, 2)]
    plus2, minus2 = far((2, -2))
    plus1, minus1, zero = far((1, -1, 0))
    plus2, minus2 = relay([plus2, minus2], nexts, parts, rows)
    slots = merge(
        [zero, along_z(plus1, -1), along_z(minus1, 1), along_z(plus2, -2), along_z(minus2, 2)],
        part,
    )
    back = [slots[0]] + [along_x(slots[d], -d) for d in range(1, NX)]
    return finish(back, part), packed[0]


def conv_part(latent, norm_gain, conv_weight, conv_bias):
    channels, _, rows, width = latent.shape
    squares = jnp.sum(jnp.square(latent.astype(jnp.float32)), axis=0)
    squares = squares + lax.ppermute(squares, "head", head_shift(0, 1))
    squares = squares + sum(
        lax.ppermute(squares, "head", head_shift(d, 0)) for d in range(1, NY)
    )
    scaled = (
        latent.astype(jnp.float32)
        * lax.rsqrt(squares / CHANNELS + norm_eps)[None]
        * norm_gain[:, None, None, None]
    )
    act = jax.nn.silu(scaled).astype(jnp.bfloat16)
    count = lax.axis_size("hist")
    forward = [(i, i + 1) for i in range(count - 1)]
    backward = [(b, a) for a, b in forward]
    low = lax.ppermute(act[:, :, -1:], "hist", forward)
    high = lax.ppermute(act[:, :, :1], "hist", backward)
    padded = jnp.pad(
        jnp.concatenate([low, act, high], axis=2), ((0, 0), (0, 0), (0, 0), (1, 1))
    )
    windows = [
        padded[:, a, b : b + rows, e : e + width]
        for a in range(3)
        for b in range(3)
        for e in range(3)
    ]
    patches = jnp.concatenate(windows, axis=0)
    flat = conv_weight.reshape(27 * channels, conv_weight.shape[4])
    terms = jnp.einsum("kyx,ko->oyx", patches, flat, preferred_element_type=jnp.float32)
    terms = terms.astype(jnp.bfloat16).reshape(NY, 2, channels, rows, width)
    core = lax.rem(lax.axis_index("head"), 2)
    y = lax.axis_index("head") // 2
    kept = lax.dynamic_index_in_dim(terms, core, 1, keepdims=False)
    given = lax.dynamic_index_in_dim(terms, 1 - core, 1, keepdims=False)
    both = kept.astype(jnp.float32) + lax.ppermute(given, "head", head_shift(0, 1)).astype(
        jnp.float32
    )
    total = lax.dynamic_index_in_dim(both, y, 0, keepdims=False)
    sent = both.astype(jnp.bfloat16)
    for d in range(1, NY):
        piece = lax.dynamic_index_in_dim(sent, lax.rem(y + d, NY), 0, keepdims=False)
        total = total + lax.ppermute(piece, "head", head_shift(d, 0)).astype(jnp.float32)
    return (total + conv_bias[:, None, None]).astype(jnp.bfloat16)


def on_device(
    queries,
    cache_keys,
    cache_values,
    hist_lengths,
    frame_bounds,
    latent,
    norm_gain,
    conv_weight,
    conv_bias,
):
    attention, packed = attention_part(
        queries, cache_keys, cache_values, hist_lengths, frame_bounds
    )
    latent, _ = lax.optimization_barrier((latent, packed))
    vae_out = conv_part(latent, norm_gain, conv_weight, conv_bias)
    return (attention, vae_out)


def solution(mesh):
    placed = (
        P("hist", "head"),
        P("hist", "head"),
        P("hist", "head"),
        P("hist"),
        P(),
        P("head", None, "hist", None),
        P("head"),
        P(None, None, None, "head", None),
        P("head"),
    )
    return jax.shard_map(
        on_device,
        mesh=mesh,
        in_specs=placed,
        out_specs=(P("hist", "head"), P("head", "hist", None)),
        check_vma=False,
    )
```

```python
import functools
import math

import jax
import jax.numpy as jnp
from jax import lax
from jax.experimental import pallas as pl
from jax.experimental.pallas import tpu as pltpu
from jax.sharding import PartitionSpec as P

HEAD_DIM = 128
CHANNELS = 384
NX = 4
NZ = 8

NEG = -1e30
LOG2E = math.log2(math.e)
norm_eps = 1e-06
VMEM = 56 << 20
SIZES = (512, 768, 1152)

ALONG_X = [[x * NZ + z for x in range(NX)] for z in range(NZ)]
ALONG_Z = [[x * NZ + z for z in range(NZ)] for x in range(NX)]

vmem = pl.BlockSpec(memory_space=pltpu.VMEM)
smem = pl.BlockSpec(memory_space=pltpu.SMEM)


def hist_shift(dx):
    return [(x * NZ + z, ((x + dx) % NX) * NZ + z) for x in range(NX) for z in range(NZ)]


def dot(a, b, dims):
    return lax.dot_general(a, b, (dims, ((), ())), preferred_element_type=jnp.float32)


def cost(micros, nbytes):
    return pl.CostEstimate(
        flops=int(micros * 1.1e9), bytes_accessed=nbytes, transcendentals=0
    )


def pack_queries_kernel(q_ref, out):
    for i in range(NX):
        out[i, :, :128] = q_ref[:, i * 128 : (i + 1) * 128]
        out[i, :, 128:] = q_ref[:, NX * 128 :]


def pack_queries(queries):
    return pl.pallas_call(
        pack_queries_kernel,
        out_shape=jax.ShapeDtypeStruct((NX, queries.shape[0], 256), jnp.bfloat16),
        cost_estimate=cost(1, 1 << 18),
        name="pack_q",
    )(queries)


def pack_cache_kernel(len_ref, k_ref, v_ref, out):
    rows = k_ref.shape[0]
    length = len_ref[0]
    row = lax.broadcasted_iota(jnp.int32, (16, 256), 0)
    tail = jnp.where(row == 0, length // 64, jnp.where(row == 1, lax.rem(length, 64), 0))
    tail = tail.astype(jnp.float32).astype(jnp.bfloat16)
    for i in range(NX):
        out[i, :rows, :128] = k_ref[:, i * 128 : (i + 1) * 128]
        out[i, :rows, 128:] = v_ref[:, i * 128 : (i + 1) * 128]
        out[i, rows:, :] = tail


def pack_cache(lengths, keys, values):
    return pl.pallas_call(
        pack_cache_kernel,
        in_specs=[smem, vmem, vmem],
        out_shape=jax.ShapeDtypeStruct((NX, keys.shape[0] + 16, 256), jnp.bfloat16),
        compiler_params=pltpu.CompilerParams(vmem_limit_bytes=VMEM),
        cost_estimate=cost(3, 7 << 20),
        name="pack_kv",
    )(lengths, keys, values)


def unit(q_of, n, group, k_of, v_of, limit, rows, acc_ref, l_ref, m_ref, c2):
    def step(low, count):
        row = lax.broadcasted_iota(jnp.int32, (count - low, 128), 0) + low
        seen = row < limit
        first = jnp.broadcast_to(k_of(0, 16).astype(jnp.float32)[:1, :], (count - low, 128))
        k = jnp.where(seen, k_of(low, count).astype(jnp.float32), first).astype(jnp.bfloat16)
        v = jnp.where(seen, v_of(low, count).astype(jnp.float32), 0.0).astype(jnp.bfloat16)
        one = jnp.where(seen, 1.0, 0.0).astype(jnp.bfloat16)
        v = jnp.concatenate([v, one], axis=1)
        if low:
            k = jnp.concatenate([k_of(0, low), k], axis=0)
            ahead = [v_of(0, low), jnp.ones((low, 128), jnp.bfloat16)]
            v = jnp.concatenate([jnp.concatenate(ahead, axis=1), v], axis=0)

        s = dot(q_of(0), k, ((1,), (1,)))
        for g in range(n):
            later = dot(q_of(g + 1), k, ((1,), (1,))) if g + 1 < n else None
            here = slice(g * group, (g + 1) * group)
            old = m_ref[here, :]
            new = jnp.maximum(old, jnp.max(s, axis=1, keepdims=True) * c2)
            p = jnp.exp2(s * c2 - new[:, :1]).astype(jnp.bfloat16)
            r = dot(p, v, ((1,), (0,)))
            a = jnp.exp2(old - new)
            acc_ref[here, :] = acc_ref[here, :] * a + r[:, :128]
            l_ref[here, :] = l_ref[here, :] * a + r[:, 128:]
            m_ref[here, :] = new
            s = later

    low = 0
    for size in SIZES + (rows,):
        pl.when((limit > low) & (limit <= size))(functools.partial(step, low, size))
        low = size


def three_parts(value):
    high = value.astype(jnp.bfloat16).astype(jnp.float32)
    rest = value - high
    mid = rest.astype(jnp.bfloat16).astype(jnp.float32)
    return [high, mid, rest - mid]


def attn_kernel(turn, part, rows, c2, len_ref, bounds_ref, q_ref, kv, k4, v4, out, *refs):
    q_buf, acc_ref, l_ref, m_ref = refs
    h = lax.axis_index("hist")
    x, z = h // NZ, lax.rem(h, NZ)
    frame = lax.rem(x + turn, NX)
    bound = bounds_ref[frame]
    for g in range(NZ):
        at = pl.multiple_of(g * NX * part + frame * part, 16)
        q_buf[g * part : (g + 1) * part, :] = q_ref[pl.ds(at, part), :]
    group = NZ * part // 2
    lane = lax.broadcasted_iota(jnp.int32, (NZ * part, 128), 1)
    table = jnp.zeros((NZ * part, 128), jnp.float32)
    for head in range(2):
        acc_ref[...] = jnp.zeros_like(acc_ref)
        l_ref[...] = jnp.zeros_like(l_ref)
        m_ref[...] = jnp.full_like(m_ref, NEG)
        add = functools.partial(
            unit,
            lambda g: q_buf[g * group : (g + 1) * group, head * 128 : (head + 1) * 128],
            2,
            group,
        )
        state = (rows, acc_ref, l_ref, m_ref, c2)
        if head == 0:

            def body(u, carry):
                tail = kv[u, rows : rows + 16, :128].astype(jnp.float32)
                row = lax.broadcasted_iota(jnp.int32, (16, 128), 0)
                high = jnp.max(jnp.where(row == 0, tail, 0.0))
                low = jnp.max(jnp.where(row == 1, tail, 0.0))
                length = (high * 64.0 + low).astype(jnp.int32)
                limit = jnp.minimum(length, bound - (u * NZ + z) * rows)
                add(
                    lambda a, b: kv[u, a:b, :128],
                    lambda a, b: kv[u, a:b, 128:],
                    limit,
                    *state,
                )
                return carry

            lax.fori_loop(0, NX, body, 0)
        else:
            limit = jnp.minimum(len_ref[0], bound - h * rows)
            add(lambda a, b: k4[a:b, :], lambda a, b: v4[a:b, :], limit, *state)
        l = jnp.maximum(l_ref[...], 1.0)
        normed = (acc_ref[...] / l).astype(jnp.bfloat16)
        for g in range(NZ):
            out[g, :part, head * 128 : (head + 1) * 128] = normed[g * part : (g + 1) * part, :]
        for k, piece in enumerate(three_parts(m_ref[...] + jnp.log2(l))):
            table = jnp.where(lane == k * 2 + head, piece, table)
    for g in range(NZ):
        piece = jnp.concatenate(
            [table[g * part : (g + 1) * part, :], jnp.zeros((128 - part, 128), jnp.float32)],
            axis=0,
        )
        out[g, part : part + 16, :128] = piece.T[:16, :].astype(jnp.bfloat16)
        out[g, part : part + 16, 128:] = jnp.zeros((16, 128), jnp.bfloat16)


def attn(turn, length, bounds, queries, kv, k4, v4, part, c2):
    rows = k4.shape[0]
    return pl.pallas_call(
        functools.partial(attn_kernel, turn, part, rows, c2),
        out_shape=jax.ShapeDtypeStruct((NZ, part + 16, 256), jnp.bfloat16),
        in_specs=[smem, smem, vmem, vmem, vmem, vmem],
        out_specs=vmem,
        scratch_shapes=[pltpu.VMEM((NZ * part, 256), jnp.bfloat16)]
        + [pltpu.VMEM((NZ * part, 128), jnp.float32)] * 3,
        compiler_params=pltpu.CompilerParams(vmem_limit_bytes=VMEM),
        cost_estimate=cost(9, 1 << 20),
        name="attn",
    )(length, bounds, queries, kv, k4, v4)


def read_log(rows16, heads, head):
    at = [k * heads + head for k in range(3)]
    return sum(rows16[a : a + 1, :] for a in at)


def weights_of(rows_list):
    top = functools.reduce(jnp.maximum, rows_list)
    raw = [jnp.exp2(r - top) for r in rows_list]
    total = functools.reduce(jnp.add, raw)
    return [r / total for r in raw], top + jnp.log2(total)


def table_of(rows_list):
    fill = jnp.zeros((128 - len(rows_list), 128), jnp.float32)
    return jnp.concatenate(rows_list + [fill], axis=0).T


def merge_z(ref, part):
    logs = [ref[s, part : part + 16, :128].astype(jnp.float32) for s in range(NZ)]
    w0, _ = weights_of([read_log(lg, 2, 0) for lg in logs])
    w1, joint = weights_of([read_log(lg, 2, 1) for lg in logs])
    table = table_of(w0 + w1)
    sums = []
    for head in range(2):
        total = jnp.zeros((part, 128), jnp.float32)
        for s in range(NZ):
            at = head * NZ + s
            data = ref[s, :part, head * 128 : (head + 1) * 128].astype(jnp.float32)
            total += table[:part, at : at + 1] * data
        sums.append(total)
    return sums, joint


def merge_kernel(part, ref, out):
    sums, joint = merge_z(ref, part)
    out[:part, :128] = sums[0].astype(jnp.bfloat16)
    out[:part, 128:] = sums[1].astype(jnp.bfloat16)
    flat = jnp.concatenate(three_parts(joint) + [jnp.zeros((13, 128), jnp.float32)], axis=0)
    out[part:, :128] = flat.astype(jnp.bfloat16)
    out[part:, 128:] = jnp.zeros((16, 128), jnp.bfloat16)


def merge(payload, part):
    return pl.pallas_call(
        functools.partial(merge_kernel, part),
        out_shape=jax.ShapeDtypeStruct((part + 16, 256), jnp.bfloat16),
        cost_estimate=cost(2, 1 << 20),
        name="merge",
    )(payload)


def finish_kernel(part, ref, *refs):
    others, out = refs[: NX - 1], refs[NX - 1]
    x = lax.axis_index("hist") // NZ
    sums, joint = merge_z(ref, part)
    logs = [joint]
    for r in others:
        logs.append(read_log(r[part : part + 16, :128].astype(jnp.float32), 1, 0))
    table = table_of(weights_of(logs)[0])
    out[:, pl.ds(pl.multiple_of(x * 128, 128), 128)] = sums[0].astype(jnp.bfloat16)
    total = table[:part, :1] * sums[1]
    for k, r in enumerate(others):
        head = lax.rem(x + NX - 1 - k, NX)
        out[:, pl.ds(pl.multiple_of(head * 128, 128), 128)] = r[:part, :128]
        total += table[:part, k + 1 : k + 2] * r[:part, 128:].astype(jnp.float32)
    out[:, NX * 128 :] = total.astype(jnp.bfloat16)


def finish(payload, others, part):
    return pl.pallas_call(
        functools.partial(finish_kernel, part),
        out_shape=jax.ShapeDtypeStruct((part, (NX + 1) * 128), jnp.bfloat16),
        cost_estimate=cost(2, 1 << 20),
        name="finish",
    )(payload, *others)


def attention_part(queries, keys, values, length, bounds):
    part = queries.shape[0]
    c2 = HEAD_DIM ** (-0.5) * LOG2E
    packed = pack_queries(queries)
    mine = lax.all_to_all(packed, "hist", 0, 0, axis_index_groups=ALONG_X)
    mine = mine.reshape(NX * part, 256)
    keys, values, _ = lax.optimization_barrier((keys, values, packed))
    cache = pack_cache(length, keys, values)
    cache, mine = lax.optimization_barrier((cache, mine))
    everyone = lax.all_gather(mine, "hist", axis=0, tiled=True, axis_index_groups=ALONG_Z)
    kv = lax.all_to_all(cache, "hist", 0, 0, axis_index_groups=ALONG_X)
    k4, v4 = keys[:, NX * 128 :], values[:, NX * 128 :]

    landed = []
    for turn in (1, 2, 3, 0):
        payload = attn(turn, length, bounds, everyone, kv, k4, v4, part, c2)
        landed.append(lax.all_to_all(payload, "hist", 0, 0, axis_index_groups=ALONG_Z))
    others = [
        lax.ppermute(merge(landed[i], part), "hist", hist_shift(i + 1)) for i in range(NX - 1)
    ]
    return finish(landed[NX - 1], others, part), packed


def conv_part(latent, norm_gain, conv_weight, conv_bias):
    channels, times, rows, width = latent.shape
    flat = latent.reshape(channels, times * rows * width)
    whole = lax.all_gather(flat, "head", axis=0, tiled=True)
    squares = jnp.sum(jnp.square(whole.astype(jnp.float32)), axis=0)
    scaled = (
        flat.astype(jnp.float32)
        * lax.rsqrt(squares / CHANNELS + norm_eps)[None]
        * norm_gain[:, None]
    )
    act = jax.nn.silu(scaled).astype(jnp.bfloat16).reshape(latent.shape)
    count = lax.axis_size("hist")
    forward = [(i, i + 1) for i in range(count - 1)]
    backward = [(b, a) for a, b in forward]
    low = lax.ppermute(act[:, :, -1:], "hist", forward)
    high = lax.ppermute(act[:, :, :1], "hist", backward)
    padded = jnp.pad(
        jnp.concatenate([low, act, high], axis=2), ((0, 0), (0, 0), (0, 0), (1, 1))
    )
    windows = [
        padded[:, a, b : b + rows, e : e + width]
        for a in range(3)
        for b in range(3)
        for e in range(3)
    ]
    patches = jnp.concatenate(windows, axis=0).reshape(27 * channels, rows * width)
    weight = conv_weight.reshape(27 * channels, conv_weight.shape[4])
    terms = jnp.einsum("kp,ko->op", patches, weight, preferred_element_type=jnp.float32)
    total = lax.psum_scatter(
        terms.astype(jnp.bfloat16), "head", scatter_dimension=0, tiled=True
    )
    out = (total.astype(jnp.float32) + conv_bias[:, None]).astype(jnp.bfloat16)
    return out.reshape(channels, rows, width)


def on_device(
    queries,
    cache_keys,
    cache_values,
    hist_lengths,
    frame_bounds,
    latent,
    norm_gain,
    conv_weight,
    conv_bias,
):
    attention, packed = attention_part(
        queries, cache_keys, cache_values, hist_lengths, frame_bounds
    )
    vae_out = conv_part(latent, norm_gain, conv_weight, conv_bias)
    return (attention, vae_out)


def solution(mesh):
    placed = (
        P("hist", "head"),
        P("hist", "head"),
        P("hist", "head"),
        P("hist"),
        P(),
        P("head", None, "hist", None),
        P("head"),
        P(None, None, None, "head", None),
        P("head"),
    )
    return jax.shard_map(
        on_device,
        mesh=mesh,
        in_specs=placed,
        out_specs=(P("hist", "head"), P("head", "hist", None)),
        check_vma=False,
    )
```

```python
import functools
import math

import jax
import jax.numpy as jnp
from jax import lax
from jax.experimental import pallas as pl
from jax.experimental.pallas import tpu as pltpu
from jax.sharding import PartitionSpec as P

HEAD_DIM = 128
CHANNELS = 384
NX = 4
NZ = 8

NEG = -1e30
LOG2E = math.log2(math.e)
norm_eps = 1e-06
VMEM = 56 << 20
SIZES = (640, 1024)

ALONG_X = [[x * NZ + z for x in range(NX)] for z in range(NZ)]
ALONG_Z = [[x * NZ + z for z in range(NZ)] for x in range(NX)]

vmem = pl.BlockSpec(memory_space=pltpu.VMEM)
smem = pl.BlockSpec(memory_space=pltpu.SMEM)


def hist_shift(dx):
    return [(x * NZ + z, ((x + dx) % NX) * NZ + z) for x in range(NX) for z in range(NZ)]


def dot(a, b, dims):
    return lax.dot_general(a, b, (dims, ((), ())), preferred_element_type=jnp.float32)


def cost(micros, nbytes):
    return pl.CostEstimate(
        flops=int(micros * 1.1e9), bytes_accessed=nbytes, transcendentals=0
    )


def pack_queries_kernel(q_ref, out, last):
    for i in range(NX):
        out[i] = q_ref[:, i * 128 : (i + 1) * 128]
    last[...] = q_ref[:, NX * 128 :]


def pack_queries(queries):
    rows = queries.shape[0]
    return pl.pallas_call(
        pack_queries_kernel,
        out_shape=[
            jax.ShapeDtypeStruct((NX, rows, 128), jnp.bfloat16),
            jax.ShapeDtypeStruct((rows, 128), jnp.bfloat16),
        ],
        cost_estimate=cost(1, 1 << 18),
        name="pack_q",
    )(queries)


def pack_cache_kernel(len_ref, k_ref, v_ref, *outs):
    x = lax.axis_index("hist") // NZ
    rows = k_ref.shape[0]
    length = len_ref[0]
    row = lax.broadcasted_iota(jnp.int32, (16, 256), 0)
    tail = jnp.where(row == 0, length // 64, jnp.where(row == 1, lax.rem(length, 64), 0))
    tail = tail.astype(jnp.float32).astype(jnp.bfloat16)
    for d, out in enumerate(outs):
        head = lax.rem(x + d, NX) if d < NX else NX
        cols = pl.ds(pl.multiple_of(head * 128, 128), 128)
        out[:rows, :128] = k_ref[:, cols]
        out[:rows, 128:] = v_ref[:, cols]
        out[rows:, :] = tail


def pack_cache(lengths, keys, values):
    rows = keys.shape[0]
    return pl.pallas_call(
        pack_cache_kernel,
        in_specs=[smem, vmem, vmem],
        out_shape=[jax.ShapeDtypeStruct((rows + 16, 256), jnp.bfloat16)] * (NX + 1),
        compiler_params=pltpu.CompilerParams(vmem_limit_bytes=VMEM),
        cost_estimate=cost(3, 7 << 20),
        name="pack_kv",
    )(lengths, keys, values)


def unit(q_of, n, group, k_of, v_of, limit, rows, acc_ref, l_ref, m_ref, c2):
    def step(low, count):
        row = lax.broadcasted_iota(jnp.int32, (count - low, 128), 0) + low
        seen = row < limit
        first = jnp.broadcast_to(k_of(0, 16).astype(jnp.float32)[:1, :], (count - low, 128))
        k = jnp.where(seen, k_of(low, count).astype(jnp.float32), first).astype(jnp.bfloat16)
        v = jnp.where(seen, v_of(low, count).astype(jnp.float32), 0.0).astype(jnp.bfloat16)
        one = jnp.where(seen, 1.0, 0.0).astype(jnp.bfloat16)
        v = jnp.concatenate([v, one], axis=1)
        if low:
            k = jnp.concatenate([k_of(0, low), k], axis=0)
            ahead = [v_of(0, low), jnp.ones((low, 128), jnp.bfloat16)]
            v = jnp.concatenate([jnp.concatenate(ahead, axis=1), v], axis=0)

        s = dot(q_of(0), k, ((1,), (1,)))
        for g in range(n):
            later = dot(q_of(g + 1), k, ((1,), (1,))) if g + 1 < n else None
            here = slice(g * group, (g + 1) * group)
            old = m_ref[here, :]
            new = jnp.maximum(old, jnp.max(s, axis=1, keepdims=True) * c2)
            p = jnp.exp2(s * c2 - new[:, :1]).astype(jnp.bfloat16)
            r = dot(p, v, ((1,), (0,)))
            a = jnp.exp2(old - new)
            acc_ref[here, :] = acc_ref[here, :] * a + r[:, :128]
            l_ref[here, :] = l_ref[here, :] * a + r[:, 128:]
            m_ref[here, :] = new
            s = later

    low = 0
    for size in SIZES + (rows,):
        pl.when((limit > low) & (limit <= size))(functools.partial(step, low, size))
        low = size


def three_parts(value):
    high = value.astype(jnp.bfloat16).astype(jnp.float32)
    rest = value - high
    mid = rest.astype(jnp.bfloat16).astype(jnp.float32)
    return [high, mid, rest - mid]


def attn_kernel(slots, part, rows, c2, bounds_ref, q_ref, *refs):
    own = slots == 2
    kv_refs, refs = refs[:NX], refs[NX:]
    count = NX
    if own:
        all_ref, refs = refs[0], refs[1:]
        kv_refs = kv_refs + tuple(all_ref.at[i] for i in range(NX))
        count = 2 * NX
    out, q_buf, kv, acc_ref, l_ref, m_ref, q_sem, kv_sems = refs
    copies = [pltpu.make_async_copy(q_ref, q_buf, q_sem)]
    for u, ref in enumerate(kv_refs):
        copies.append(pltpu.make_async_copy(ref, kv.at[u], kv_sems.at[u]))
    for c in copies:
        c.start()
    acc_ref[...] = jnp.zeros_like(acc_ref)
    l_ref[...] = jnp.zeros_like(l_ref)
    m_ref[...] = jnp.full_like(m_ref, NEG)
    h = lax.axis_index("hist")
    x, z = h // NZ, lax.rem(h, NZ)
    many = NZ // 2
    for c in copies:
        c.wait()

    def body(step, carry):
        if own:
            u, slot = step, step // NX
            block_x = jnp.where(slot == 0, lax.rem(x - u + NX, NX), u - NX)
            frame = x
        else:
            u, slot = step // slots, lax.rem(step, slots)
            block_x = lax.rem(x - u + NX, NX)
            frame = lax.rem(x + 1 + slot, NX)
        tail = kv[u, rows : rows + 16, :128].astype(jnp.float32)
        row = lax.broadcasted_iota(jnp.int32, (16, 128), 0)
        high = jnp.max(jnp.where(row == 0, tail, 0.0))
        low = jnp.max(jnp.where(row == 1, tail, 0.0))
        length = (high * 64.0 + low).astype(jnp.int32)
        at = pl.ds(pl.multiple_of(slot * part, 16), part)
        unit(
            lambda g: q_buf[g * many : (g + 1) * many, at, :].reshape(many * part, 128),
            2,
            many * part,
            lambda a, b: kv[u, a:b, :128],
            lambda a, b: kv[u, a:b, 128:],
            jnp.minimum(length, bounds_ref[frame] - (block_x * NZ + z) * rows),
            rows,
            acc_ref.at[slot],
            l_ref.at[slot],
            m_ref.at[slot],
            c2,
        )
        return carry

    lax.fori_loop(0, slots * NX, body, 0)
    lane = lax.broadcasted_iota(jnp.int32, (part, 128), 1)
    fill = jnp.zeros((128 - part, 128), jnp.float32)
    empty = jnp.zeros((10, 128), jnp.float32)
    for slot in range(slots):
        base = slot * (part + 16)
        for g in range(NZ):
            here = slice(g * part, (g + 1) * part)
            out[g, base : base + part, :] = acc_ref[slot, here, :].astype(jnp.bfloat16)
            table = jnp.where(lane == 0, m_ref[slot, here, :], l_ref[slot, here, :])
            flat = jnp.concatenate([table, fill], axis=0).T[:2, :]
            flat = jnp.concatenate(three_parts(flat) + [empty], axis=0)
            out[g, base + part : base + part + 16, :] = flat.astype(jnp.bfloat16)


def attn(bounds, queries, kvs, part, c2):
    rows = kvs[0].shape[0] - 16
    slots = queries.shape[1] // part
    count = NX * (len(kvs) - NX + 1)
    anys = pl.BlockSpec(memory_space=pl.ANY)
    return pl.pallas_call(
        functools.partial(attn_kernel, slots, part, rows, c2),
        out_shape=jax.ShapeDtypeStruct((NZ, slots * (part + 16), 128), jnp.bfloat16),
        in_specs=[smem, anys] + [anys] * len(kvs),
        out_specs=vmem,
        scratch_shapes=[
            pltpu.VMEM((NZ, slots * part, 128), jnp.bfloat16),
            pltpu.VMEM((count, rows + 16, 256), jnp.bfloat16),
        ]
        + [pltpu.VMEM((slots, NZ * part, 128), jnp.float32)] * 3
        + [pltpu.SemaphoreType.DMA, pltpu.SemaphoreType.DMA((count,))],
        compiler_params=pltpu.CompilerParams(vmem_limit_bytes=VMEM),
        cost_estimate=cost(8 * slots, 1 << 20),
        name="attn",
    )(bounds, queries, *kvs)


def stat(rows16, count, which):
    at = [k * count + which for k in range(3)]
    return sum(rows16[a : a + 1, :] for a in at)


def merge_z(ref, part, slot):
    base = slot * (part + 16)
    under = slice(base + part, base + part + 16)
    stats = [ref[s, under, :].astype(jnp.float32) for s in range(NZ)]
    tops = [stat(st, 2, 0) for st in stats]
    top = functools.reduce(jnp.maximum, tops)
    raw = [jnp.exp2(t - top) for t in tops]
    total = functools.reduce(jnp.add, [r * stat(st, 2, 1) for r, st in zip(raw, stats)])
    total = jnp.maximum(total, 1.0)
    fill = jnp.zeros((128 - NZ, 128), jnp.float32)
    table = jnp.concatenate([r / total for r in raw] + [fill], axis=0).T
    out = jnp.zeros((part, 128), jnp.float32)
    for s in range(NZ):
        out += table[:part, s : s + 1] * ref[s, base : base + part, :].astype(jnp.float32)
    return out.astype(jnp.bfloat16)


def merge_kernel(part, ref, *outs):
    for slot, out in enumerate(outs):
        out[...] = merge_z(ref, part, slot)


def merge(payload, part):
    return pl.pallas_call(
        functools.partial(merge_kernel, part),
        out_shape=[jax.ShapeDtypeStruct((part, 128), jnp.bfloat16)] * (NX - 1),
        cost_estimate=cost(2, 1 << 20),
        name="merge",
    )(payload)


def finish_kernel(part, ref, *refs):
    others, out = refs[: NX - 1], refs[NX - 1]
    x = lax.axis_index("hist") // NZ
    out[:, pl.ds(pl.multiple_of(x * 128, 128), 128)] = merge_z(ref, part, 0)
    out[:, NX * 128 :] = merge_z(ref, part, 1)
    for k, r in enumerate(others):
        head = lax.rem(x + NX - 1 - k, NX)
        out[:, pl.ds(pl.multiple_of(head * 128, 128), 128)] = r[...]


def finish(payload, others, part):
    return pl.pallas_call(
        functools.partial(finish_kernel, part),
        out_shape=jax.ShapeDtypeStruct((part, (NX + 1) * 128), jnp.bfloat16),
        cost_estimate=cost(2, 1 << 20),
        name="finish",
    )(payload, *others)


def exchange(value, axis, groups=None):
    return lax.all_to_all(value, axis, 0, 0, axis_index_groups=groups)


def to_all_z(value):
    return exchange(jnp.broadcast_to(value[None], (NZ,) + value.shape), "hist", ALONG_Z)


def attention_part(queries, keys, values, length, bounds, conv):
    part = queries.shape[0]
    c2 = HEAD_DIM ** (-0.5) * LOG2E
    x = lax.axis_index("hist") // NZ
    packed, last = pack_queries(queries)
    mine = exchange(packed, "hist", ALONG_X)
    keys, values, _ = lax.optimization_barrier((keys, values, packed))
    cache = pack_cache(length, keys, values)
    kvs = [lax.ppermute(cache[d], "hist", hist_shift(d)) for d in range(1, NX)]
    kvs = [cache[0]] + kvs
    mine, _ = lax.optimization_barrier((mine, cache[0]))
    order = lax.dynamic_slice_in_dim(jnp.concatenate([mine, mine]), x + 1, NX, 0)
    foreign = to_all_z(order[: NX - 1].reshape((NX - 1) * part, 128))
    terms = conv()
    kvs, terms, foreign = lax.optimization_barrier((kvs, terms, foreign))
    last_cache, own, _ = lax.optimization_barrier(
        (cache[NX], jnp.concatenate([order[NX - 1], last], axis=0), foreign)
    )
    own = to_all_z(own)
    every = lax.all_gather(last_cache, "hist", axis=0, axis_index_groups=ALONG_X)

    landed = exchange(attn(bounds, foreign, kvs, part, c2), "hist", ALONG_Z)
    landed_own = exchange(attn(bounds, own, kvs + [every], part, c2), "hist", ALONG_Z)
    others = [
        lax.ppermute(r, "hist", hist_shift(i + 1)) for i, r in enumerate(merge(landed, part))
    ]
    return finish(landed_own, others, part), terms


def once(fun, *args):
    shapes = jax.eval_shape(fun, *args)
    turns = 1 + lax.axis_index("hist") // lax.axis_size("hist")

    def body(_, carry):
        return lax.optimization_barrier((carry[0], fun(*carry[0])))

    return lax.fori_loop(0, turns, body, (args, jnp.zeros(shapes.shape, shapes.dtype)))[1]


def conv_terms(latent, norm_gain, conv_weight):
    channels, times, rows, width = latent.shape
    flat = latent.reshape(channels, times * rows * width)
    whole = lax.all_gather(flat, "head", axis=0, tiled=True)

    def activate(flat, whole, norm_gain):
        squares = jnp.sum(jnp.square(whole.astype(jnp.float32)), axis=0)
        scaled = (
            flat.astype(jnp.float32)
            * lax.rsqrt(squares / CHANNELS + norm_eps)[None]
            * norm_gain[:, None]
        )
        return jax.nn.silu(scaled).astype(jnp.bfloat16).reshape(latent.shape)

    act = once(activate, flat, whole, norm_gain)
    count = lax.axis_size("hist")
    forward = [(i, i + 1) for i in range(count - 1)]
    backward = [(b, a) for a, b in forward]
    low = lax.ppermute(act[:, :, -1:], "hist", forward)
    high = lax.ppermute(act[:, :, :1], "hist", backward)

    def multiply(low, act, high, conv_weight):
        padded = jnp.pad(
            jnp.concatenate([low, act, high], axis=2), ((0, 0), (0, 0), (0, 0), (1, 1))
        )
        windows = [
            padded[:, a, b : b + rows, e : e + width]
            for a in range(3)
            for b in range(3)
            for e in range(3)
        ]
        patches = jnp.concatenate(windows, axis=0)
        weight = conv_weight.reshape(27 * channels, conv_weight.shape[4])
        terms = jnp.einsum("kyx,ko->oyx", patches, weight, preferred_element_type=jnp.float32)
        return terms.astype(jnp.bfloat16).reshape(-1, rows * width)

    return once(multiply, low, act, high, conv_weight)


def conv_sum(terms, conv_bias, shape):
    total = lax.psum_scatter(terms, "head", scatter_dimension=0, tiled=True)
    out = (total.astype(jnp.float32) + conv_bias[:, None]).astype(jnp.bfloat16)
    return out.reshape(shape)


def on_device(
    queries,
    cache_keys,
    cache_values,
    hist_lengths,
    frame_bounds,
    latent,
    norm_gain,
    conv_weight,
    conv_bias,
):
    attention, terms = attention_part(
        queries,
        cache_keys,
        cache_values,
        hist_lengths,
        frame_bounds,
        lambda: conv_terms(latent, norm_gain, conv_weight),
    )
    shape = (latent.shape[0], latent.shape[2], latent.shape[3])
    return (attention, conv_sum(terms, conv_bias, shape))


def solution(mesh):
    placed = (
        P("hist", "head"),
        P("hist", "head"),
        P("hist", "head"),
        P("hist"),
        P(),
        P("head", None, "hist", None),
        P("head"),
        P(None, None, None, "head", None),
        P("head"),
    )
    return jax.shard_map(
        on_device,
        mesh=mesh,
        in_specs=placed,
        out_specs=(P("hist", "head"), P("head", "hist", None)),
        check_vma=False,
    )
```

```python
import functools
import math

import jax
import jax.numpy as jnp
from jax import lax
from jax.experimental import pallas as pl
from jax.experimental.pallas import tpu as pltpu
from jax.sharding import PartitionSpec as P

HEAD_DIM = 128
CHANNELS = 384
NX = 4
NZ = 8
NY = 4

NEG = -1e30
LOG2E = math.log2(math.e)
norm_eps = 1e-06
VMEM = 56 << 20
SIZES = (640, 1024)

HIST = ("x", "z")

vmem = pl.BlockSpec(memory_space=pltpu.VMEM)
smem = pl.BlockSpec(memory_space=pltpu.SMEM)


def head_shift(dy, flip):
    return [
        (y * 2 + c, ((y + dy) % NY) * 2 + (c ^ flip)) for y in range(NY) for c in range(2)
    ]


def head_swap(bit):
    return [(i, i ^ bit) for i in range(2 * NY)]


def dot(a, b, dims):
    return lax.dot_general(a, b, (dims, ((), ())), preferred_element_type=jnp.float32)


def cost(micros, nbytes):
    return pl.CostEstimate(
        flops=int(micros * 1.1e9), bytes_accessed=nbytes, transcendentals=0
    )


def pack_queries_kernel(q_ref, out, last):
    for i in range(NX):
        out[i] = q_ref[:, i * 128 : (i + 1) * 128]
    last[...] = q_ref[:, NX * 128 :]


def pack_queries(queries):
    rows = queries.shape[0]
    return pl.pallas_call(
        pack_queries_kernel,
        out_shape=[
            jax.ShapeDtypeStruct((NX, rows, 128), jnp.bfloat16),
            jax.ShapeDtypeStruct((rows, 128), jnp.bfloat16),
        ],
        cost_estimate=cost(1, 1 << 18),
        name="pack_q",
    )(queries)


def columns(head):
    return pl.ds(pl.multiple_of(head * 128, 128), 128)


def pack_cache_kernel(len_ref, k_ref, v_ref, *outs):
    x = lax.axis_index("x")
    rows = k_ref.shape[0]
    length = len_ref[0]
    row = lax.broadcasted_iota(jnp.int32, (16, 256), 0)
    tail = jnp.where(row == 0, length // 64, jnp.where(row == 1, lax.rem(length, 64), 0))
    tail = tail.astype(jnp.float32).astype(jnp.bfloat16)
    for d, out in enumerate(outs):
        cols = columns(lax.rem(x + d, NX) if d < NX else NX)
        out[:rows, :128] = k_ref[:, cols]
        out[:rows, 128:] = v_ref[:, cols]
        out[rows:, :] = tail


def pack_cache(lengths, keys, values):
    shape = jax.ShapeDtypeStruct((keys.shape[0] + 16, 256), jnp.bfloat16)
    return pl.pallas_call(
        pack_cache_kernel,
        in_specs=[smem, vmem, vmem],
        out_shape=[shape] * (NX + 1),
        compiler_params=pltpu.CompilerParams(vmem_limit_bytes=VMEM),
        cost_estimate=cost(3, 7 << 20),
        name="pack_kv",
    )(lengths, keys, values)


def unit(q_of, n, group, k_of, v_of, limit, rows, acc_ref, l_ref, m_ref, c2):
    def step(low, count):
        row = lax.broadcasted_iota(jnp.int32, (count - low, 128), 0) + low
        seen = row < limit
        first = jnp.broadcast_to(k_of(0, 16).astype(jnp.float32)[:1, :], (count - low, 128))
        k = jnp.where(seen, k_of(low, count).astype(jnp.float32), first).astype(jnp.bfloat16)
        v = jnp.where(seen, v_of(low, count).astype(jnp.float32), 0.0).astype(jnp.bfloat16)
        one = jnp.where(seen, 1.0, 0.0).astype(jnp.bfloat16)
        v = jnp.concatenate([v, one], axis=1)
        if low:
            k = jnp.concatenate([k_of(0, low), k], axis=0)
            ahead = [v_of(0, low), jnp.ones((low, 128), jnp.bfloat16)]
            v = jnp.concatenate([jnp.concatenate(ahead, axis=1), v], axis=0)

        s = dot(q_of(0), k, ((1,), (1,)))
        for g in range(n):
            later = dot(q_of(g + 1), k, ((1,), (1,))) if g + 1 < n else None
            here = slice(g * group, (g + 1) * group)
            old = m_ref[here, :]
            new = jnp.maximum(old, jnp.max(s, axis=1, keepdims=True) * c2)
            p = jnp.exp2(s * c2 - new[:, :1]).astype(jnp.bfloat16)
            r = dot(p, v, ((1,), (0,)))
            a = jnp.exp2(old - new)
            acc_ref[here, :] = acc_ref[here, :] * a + r[:, :128]
            l_ref[here, :] = l_ref[here, :] * a + r[:, 128:]
            m_ref[here, :] = new
            s = later

    low = 0
    for size in SIZES + (rows,):
        pl.when((limit > low) & (limit <= size))(functools.partial(step, low, size))
        low = size


def three_parts(value):
    high = value.astype(jnp.bfloat16).astype(jnp.float32)
    rest = value - high
    mid = rest.astype(jnp.bfloat16).astype(jnp.float32)
    return [high, mid, rest - mid]


def attn_kernel(slots, part, rows, c2, bounds_ref, q_ref, *refs):
    own = slots == 2
    count = 2 * NX if own else NX
    kv_refs, refs = refs[:count], refs[count:]
    out, q_buf, kv, tails, lens, acc_ref, l_ref, m_ref, q_sem, kv_sems, tail_sems = refs
    first = (NX - 1) * part if own else 0
    small = []
    for u, ref in enumerate(kv_refs):
        there = tails.at[u]
        small.append(pltpu.make_async_copy(ref.at[pl.ds(rows, 16), :], there, tail_sems.at[u]))
    for c in small:
        c.start()
    q_copy = pltpu.make_async_copy(q_ref.at[:, pl.ds(first, slots * part), :], q_buf, q_sem)
    q_copy.start()
    for u, ref in enumerate(kv_refs):
        pltpu.make_async_copy(ref, kv.at[u], kv_sems.at[u]).start()
    acc_ref[...] = jnp.zeros_like(acc_ref)
    l_ref[...] = jnp.zeros_like(l_ref)
    m_ref[...] = jnp.full_like(m_ref, NEG)
    x, z = lax.axis_index("x"), lax.axis_index("z")
    many = NZ // 2

    def kv_copy(u):
        return pltpu.make_async_copy(kv_refs[0], kv.at[u], kv_sems.at[u])

    row = lax.broadcasted_iota(jnp.int32, (16, 128), 0)
    for u, c in enumerate(small):
        c.wait()
        tail = tails[u, :, :128].astype(jnp.float32)
        high = jnp.max(jnp.where(row == 0, tail, 0.0))
        low = jnp.max(jnp.where(row == 1, tail, 0.0))
        lens[u] = (high * 64.0 + low).astype(jnp.int32)
    q_copy.wait()

    def body(step, carry):
        if own:
            u, slot, frame = step, step // NX, x
            kv_copy(u).wait()
        else:
            u, slot = step // slots, lax.rem(step, slots)
            frame = lax.rem(x + 1 + slot, NX)
            pl.when(slot == 0)(lambda: kv_copy(u).wait())
        block = lax.rem(x + NX - lax.rem(u, NX), NX) * NZ + z
        at = pl.ds(pl.multiple_of(slot * part, 16), part)
        unit(
            lambda g: q_buf[g * many : (g + 1) * many, at, :].reshape(many * part, 128),
            2,
            many * part,
            lambda a, b: kv[u, a:b, :128],
            lambda a, b: kv[u, a:b, 128:],
            jnp.minimum(lens[u], bounds_ref[frame] - block * rows),
            rows,
            acc_ref.at[slot],
            l_ref.at[slot],
            m_ref.at[slot],
            c2,
        )
        return carry

    lax.fori_loop(0, slots * NX, body, 0)
    lane = lax.broadcasted_iota(jnp.int32, (part, 128), 1)
    fill = jnp.zeros((128 - part, 128), jnp.float32)
    under = slots * part
    empty = jnp.zeros((16 - 5 * slots, 128), jnp.float32)
    for g in range(NZ):
        here = slice(g * part, (g + 1) * part)
        table = jnp.zeros((part, 128), jnp.float32)
        for slot in range(slots):
            out[g, slot * part : (slot + 1) * part, :] = acc_ref[slot, here, :].astype(jnp.bfloat16)
            table = jnp.where(lane == slot, m_ref[slot, here, :], table)
            table = jnp.where(lane == slots + slot, l_ref[slot, here, :], table)
        flat = jnp.concatenate([table, fill], axis=0).T
        pieces = three_parts(flat[:slots, :]) + three_parts(flat[slots : 2 * slots, :])[:2]
        flat = jnp.concatenate(pieces + [empty], axis=0)
        out[g, under : under + 16, :] = flat.astype(jnp.bfloat16)


def attn(bounds, queries, kvs, part, c2):
    rows = kvs[0].shape[0] - 16
    slots = NX - 1 if len(kvs) == NX else 2
    anys = pl.BlockSpec(memory_space=pl.ANY)
    return pl.pallas_call(
        functools.partial(attn_kernel, slots, part, rows, c2),
        out_shape=jax.ShapeDtypeStruct((NZ, slots * part + 16, 128), jnp.bfloat16),
        in_specs=[smem, anys] + [anys] * len(kvs),
        out_specs=vmem,
        scratch_shapes=[
            pltpu.VMEM((NZ, slots * part, 128), jnp.bfloat16),
            pltpu.VMEM((len(kvs), rows + 16, 256), jnp.bfloat16),
            pltpu.VMEM((len(kvs), 16, 256), jnp.bfloat16),
            pltpu.SMEM((len(kvs),), jnp.int32),
        ]
        + [pltpu.VMEM((slots, NZ * part, 128), jnp.float32)] * 3
        + [pltpu.SemaphoreType.DMA] + [pltpu.SemaphoreType.DMA((len(kvs),))] * 2,
        compiler_params=pltpu.CompilerParams(vmem_limit_bytes=VMEM),
        cost_estimate=cost(8 * slots, 1 << 20),
        name="attn",
    )(bounds, queries, *kvs)


def merge_z(ref, part, slots, slot):
    under = slice(slots * part, slots * part + 16)
    tops, totals = [], []
    for s in range(NZ):
        rows16 = ref[s, under, :].astype(jnp.float32)
        pieces = [rows16[k * slots + slot : k * slots + slot + 1, :] for k in range(5)]
        tops.append(pieces[0] + pieces[1] + pieces[2])
        totals.append(pieces[3] + pieces[4])
    top = functools.reduce(jnp.maximum, tops)
    raw = [jnp.exp2(t - top) for t in tops]
    total = functools.reduce(jnp.add, [r * t for r, t in zip(raw, totals)])
    total = jnp.maximum(total, 1.0)
    fill = jnp.zeros((128 - NZ, 128), jnp.float32)
    table = jnp.concatenate([r / total for r in raw] + [fill], axis=0).T
    out = jnp.zeros((part, 128), jnp.float32)
    for s in range(NZ):
        data = ref[s, slot * part : (slot + 1) * part, :].astype(jnp.float32)
        out += table[:part, s : s + 1] * data
    return out.astype(jnp.bfloat16)


def merge_kernel(part, ref, *outs):
    for slot, out in enumerate(outs):
        out[...] = merge_z(ref, part, len(outs), slot)


def merge(payload, part):
    return pl.pallas_call(
        functools.partial(merge_kernel, part),
        out_shape=[jax.ShapeDtypeStruct((part, 128), jnp.bfloat16)] * (NX - 1),
        cost_estimate=cost(2, 1 << 20),
        name="merge",
    )(payload)


def finish_kernel(part, ref, *refs):
    others, out = refs[: NX - 1], refs[NX - 1]
    x = lax.axis_index("x")
    out[:, pl.ds(pl.multiple_of(x * 128, 128), 128)] = merge_z(ref, part, 2, 0)
    out[:, NX * 128 :] = merge_z(ref, part, 2, 1)
    for k, r in enumerate(others):
        head = lax.rem(x + NX - 1 - k, NX)
        out[:, pl.ds(pl.multiple_of(head * 128, 128), 128)] = r[...]


def finish(payload, others, part):
    return pl.pallas_call(
        functools.partial(finish_kernel, part),
        out_shape=jax.ShapeDtypeStruct((part, (NX + 1) * 128), jnp.bfloat16),
        cost_estimate=cost(2, 1 << 20),
        name="finish",
    )(payload, *others)


def exchange(value, axis):
    return lax.all_to_all(value, axis, 0, 0)


def along_x(value, dx):
    return lax.ppermute(value, "x", [(x, (x + dx) % NX) for x in range(NX)])


def attention_part(queries, keys, values, length, bounds, conv):
    part = queries.shape[0]
    c2 = HEAD_DIM ** (-0.5) * LOG2E
    x = lax.axis_index("x")
    packed, last = pack_queries(queries)
    mine = exchange(packed, "x")
    keys, values, _ = lax.optimization_barrier((keys, values, packed))
    cache = pack_cache(length, keys, values)
    kvs = [cache[0]] + [along_x(cache[d], d) for d in range(1, NX)]
    order = lax.dynamic_slice_in_dim(jnp.concatenate([mine, mine]), x + 1, NX, 0)
    order = jnp.concatenate([order.reshape(NX * part, 128), last], axis=0)
    order, _ = lax.optimization_barrier((order, cache[0]))
    everyone = exchange(jnp.broadcast_to(order[None], (NZ,) + order.shape), "z")
    last, kvs, terms, everyone = lax.optimization_barrier(
        (cache[NX], kvs, conv(cache[0]), everyone)
    )
    lasts = [last] + [along_x(last, d) for d in range(1, NX)]

    landed = exchange(attn(bounds, everyone, kvs, part, c2), "z")
    landed_own = exchange(attn(bounds, everyone, kvs + lasts, part, c2), "z")
    others = [along_x(r, i + 1) for i, r in enumerate(merge(landed, part))]
    return finish(landed_own, others, part), terms


def once(fun, *args):
    shapes = jax.eval_shape(fun, *args)
    turns = 1 + lax.axis_index("x") // NX

    def body(_, carry):
        return lax.optimization_barrier((carry[0], fun(*carry[0])))

    return lax.fori_loop(0, turns, body, (args, jnp.zeros(shapes.shape, shapes.dtype)))[1]


def conv_terms(low, latent, high, norm_gain, conv_weight):
    channels, _, rows, width = latent.shape
    wide = jnp.concatenate([low, latent, high], axis=2)
    squares = jnp.sum(jnp.square(wide.astype(jnp.float32)), axis=0)
    for bit in (1, 2, 4):
        squares = squares + lax.ppermute(squares, "head", head_swap(bit))
    scaled = (
        wide.astype(jnp.float32)
        * lax.rsqrt(squares / CHANNELS + norm_eps)[None]
        * norm_gain[:, None, None, None]
    )
    act = jax.nn.silu(scaled).astype(jnp.bfloat16)
    padded = jnp.pad(act, ((0, 0), (0, 0), (0, 0), (1, 1)))
    windows = [
        padded[:, a, b : b + rows, e : e + width]
        for a in range(3)
        for b in range(3)
        for e in range(3)
    ]
    patches = jnp.concatenate(windows, axis=0)
    weight = conv_weight.reshape(27 * channels, conv_weight.shape[4])
    terms = jnp.einsum("kyx,ko->oyx", patches, weight, preferred_element_type=jnp.float32)
    return terms.astype(jnp.bfloat16).reshape(-1, rows * width)


def neighbour_rows(latent):
    count = lax.axis_size(HIST)
    forward = [(i, i + 1) for i in range(count - 1)]
    backward = [(b, a) for a, b in forward]
    low = lax.ppermute(latent[:, :, -1:], HIST, forward)
    high = lax.ppermute(latent[:, :, :1], HIST, backward)
    return low, high


def conv_sum(terms, conv_bias, shape):
    terms = terms.reshape(NY, 2, shape[0], -1)
    core = lax.rem(lax.axis_index("head"), 2)
    y = lax.axis_index("head") // 2
    kept = lax.dynamic_index_in_dim(terms, core, 1, keepdims=False)
    given = lax.dynamic_index_in_dim(terms, 1 - core, 1, keepdims=False)
    given = lax.ppermute(given, "head", head_swap(1))
    both = kept.astype(jnp.float32) + given.astype(jnp.float32)
    total = lax.dynamic_index_in_dim(both, y, 0, keepdims=False)
    sent = both.astype(jnp.bfloat16)
    for d in range(1, NY):
        piece = lax.dynamic_index_in_dim(sent, lax.rem(y + d, NY), 0, keepdims=False)
        total = total + lax.ppermute(piece, "head", head_shift(d, 0)).astype(jnp.float32)
    out = (total + conv_bias[:, None]).astype(jnp.bfloat16)
    return out.reshape(shape)


def on_device(
    queries,
    cache_keys,
    cache_values,
    hist_lengths,
    frame_bounds,
    latent,
    norm_gain,
    conv_weight,
    conv_bias,
):
    low, high = neighbour_rows(latent)
    attention, terms = attention_part(
        queries,
        cache_keys,
        cache_values,
        hist_lengths,
        frame_bounds,
        lambda after: once(
            conv_terms,
            low,
            lax.optimization_barrier((latent, after))[0],
            high,
            norm_gain,
            conv_weight,
        ),
    )
    shape = (latent.shape[0], latent.shape[2], latent.shape[3])
    return (attention, conv_sum(terms, conv_bias, shape))


def solution(mesh):
    split = jax.sharding.Mesh(
        mesh.devices.reshape(NX, NZ, mesh.shape["head"]), ("x", "z", "head")
    )
    hist = ("x", "z")
    placed = (
        P(hist, "head"),
        P(hist, "head"),
        P(hist, "head"),
        P(hist),
        P(),
        P("head", None, hist, None),
        P("head"),
        P(None, None, None, "head", None),
        P("head"),
    )
    return jax.shard_map(
        on_device,
        mesh=split,
        in_specs=placed,
        out_specs=(P(hist, "head"), P("head", hist, None)),
        check_vma=False,
    )
```

```python
import functools
import math

import jax
import jax.numpy as jnp
from jax import lax
from jax.experimental import pallas as pl
from jax.experimental.pallas import tpu as pltpu
from jax.sharding import PartitionSpec as P

HEAD_DIM = 128
CHANNELS = 384
NX = 4
NZ = 8
NY = 4

NEG = -1e30
LOG2E = math.log2(math.e)
norm_eps = 1e-06
VMEM = 56 << 20
SIZES = (512, 768, 1024, 1152)

HIST = ("x", "z")

vmem = pl.BlockSpec(memory_space=pltpu.VMEM)
smem = pl.BlockSpec(memory_space=pltpu.SMEM)


def head_shift(dy, flip):
    return [
        (y * 2 + c, ((y + dy) % NY) * 2 + (c ^ flip)) for y in range(NY) for c in range(2)
    ]


def head_swap(bit):
    return [(i, i ^ bit) for i in range(2 * NY)]


def dot(a, b, dims):
    return lax.dot_general(a, b, (dims, ((), ())), preferred_element_type=jnp.float32)


def cost(micros, nbytes):
    return pl.CostEstimate(
        flops=int(micros * 1.1e9), bytes_accessed=nbytes, transcendentals=0
    )


def pack_queries_kernel(q_ref, out, last):
    for i in range(NX):
        out[i] = q_ref[:, i * 128 : (i + 1) * 128]
    last[...] = q_ref[:, NX * 128 :]


def pack_queries(queries):
    rows = queries.shape[0]
    return pl.pallas_call(
        pack_queries_kernel,
        out_shape=[
            jax.ShapeDtypeStruct((NX, rows, 128), jnp.bfloat16),
            jax.ShapeDtypeStruct((rows, 128), jnp.bfloat16),
        ],
        cost_estimate=cost(1, 1 << 18),
        name="pack_q",
    )(queries)


def columns(head):
    return pl.ds(pl.multiple_of(head * 128, 128), 128)


def pack_cache_kernel(len_ref, k_ref, v_ref, *outs):
    x = lax.axis_index("x")
    rows = k_ref.shape[0]
    length = len_ref[0]
    row = lax.broadcasted_iota(jnp.int32, (16, 256), 0)
    tail = jnp.where(row == 0, length // 64, jnp.where(row == 1, lax.rem(length, 64), 0))
    tail = tail.astype(jnp.float32).astype(jnp.bfloat16)
    for d, out in enumerate(outs):
        cols = columns(lax.rem(x + d, NX) if d < NX else NX)
        out[:rows, :128] = k_ref[:, cols]
        out[:rows, 128:] = v_ref[:, cols]
        out[rows:, :] = tail


def pack_cache(lengths, keys, values):
    shape = jax.ShapeDtypeStruct((keys.shape[0] + 16, 256), jnp.bfloat16)
    return pl.pallas_call(
        pack_cache_kernel,
        in_specs=[smem, vmem, vmem],
        out_shape=[shape] * (NX + 1),
        compiler_params=pltpu.CompilerParams(vmem_limit_bytes=VMEM),
        cost_estimate=cost(3, 7 << 20),
        name="pack_kv",
    )(lengths, keys, values)


def unit(q_of, n, group, k_of, v_of, limit, rows, acc_ref, l_ref, m_ref, c2):
    def step(low, count):
        row = lax.broadcasted_iota(jnp.int32, (count - low, 128), 0) + low
        seen = row < limit
        first = jnp.broadcast_to(k_of(0, 16).astype(jnp.float32)[:1, :], (count - low, 128))
        k = jnp.where(seen, k_of(low, count).astype(jnp.float32), first).astype(jnp.bfloat16)
        v = jnp.where(seen, v_of(low, count).astype(jnp.float32), 0.0).astype(jnp.bfloat16)
        one = jnp.where(seen, 1.0, 0.0).astype(jnp.bfloat16)
        v = jnp.concatenate([v, one], axis=1)
        if low:
            k = jnp.concatenate([k_of(0, low), k], axis=0)
            ahead = [v_of(0, low), jnp.ones((low, 128), jnp.bfloat16)]
            v = jnp.concatenate([jnp.concatenate(ahead, axis=1), v], axis=0)

        s = dot(q_of(0), k, ((1,), (1,)))
        for g in range(n):
            later = dot(q_of(g + 1), k, ((1,), (1,))) if g + 1 < n else None
            here = slice(g * group, (g + 1) * group)
            old = m_ref[here, :]
            new = jnp.maximum(old, jnp.max(s, axis=1, keepdims=True) * c2)
            p = jnp.exp2(s * c2 - jnp.concatenate([new] * (count // 128), axis=1)).astype(jnp.bfloat16)
            r = dot(p, v, ((1,), (0,)))
            a = jnp.exp2(old - new)
            acc_ref[here, :] = acc_ref[here, :] * a + r[:, :128]
            l_ref[here, :] = l_ref[here, :] * a + r[:, 128:]
            m_ref[here, :] = new
            s = later

    low = 0
    for size in SIZES + (-(-rows // 128) * 128,):
        pl.when((limit > low) & (limit <= size))(functools.partial(step, low, size))
        low = size


def three_parts(value):
    high = value.astype(jnp.bfloat16).astype(jnp.float32)
    rest = value - high
    mid = rest.astype(jnp.bfloat16).astype(jnp.float32)
    return [high, mid, rest - mid]


def attn_kernel(slots, part, rows, c2, bounds_ref, q_ref, *refs):
    own = slots == 2
    count = 2 * NX if own else NX
    kv_refs, refs = refs[:count], refs[count:]
    out, q_buf, kv, tails, lens, acc_ref, l_ref, m_ref, q_sem, kv_sems, tail_sems = refs
    first = (NX - 1) * part if own else 0
    small = []
    for u, ref in enumerate(kv_refs):
        there = tails.at[u]
        small.append(pltpu.make_async_copy(ref.at[pl.ds(rows, 16), :], there, tail_sems.at[u]))
    for c in small:
        c.start()
    q_copy = pltpu.make_async_copy(q_ref.at[:, pl.ds(first, slots * part), :], q_buf, q_sem)
    q_copy.start()
    for u, ref in enumerate(kv_refs):
        pltpu.make_async_copy(ref, kv.at[u, pl.ds(0, rows + 16), :], kv_sems.at[u]).start()
    acc_ref[...] = jnp.zeros_like(acc_ref)
    l_ref[...] = jnp.zeros_like(l_ref)
    m_ref[...] = jnp.full_like(m_ref, NEG)
    x, z = lax.axis_index("x"), lax.axis_index("z")
    many = NZ // 2

    def kv_copy(u):
        return pltpu.make_async_copy(kv_refs[0], kv.at[u, pl.ds(0, rows + 16), :], kv_sems.at[u])

    row = lax.broadcasted_iota(jnp.int32, (16, 128), 0)
    for u, c in enumerate(small):
        c.wait()
        tail = tails[u, :, :128].astype(jnp.float32)
        high = jnp.max(jnp.where(row == 0, tail, 0.0))
        low = jnp.max(jnp.where(row == 1, tail, 0.0))
        lens[u] = (high * 64.0 + low).astype(jnp.int32)
    q_copy.wait()

    def body(step, carry):
        if own:
            u, slot, frame = step, step // NX, x
            kv_copy(u).wait()
        else:
            u, slot = step // slots, lax.rem(step, slots)
            frame = lax.rem(x + 1 + slot, NX)
            pl.when(slot == 0)(lambda: kv_copy(u).wait())
        block = lax.rem(x + NX - lax.rem(u, NX), NX) * NZ + z
        at = pl.ds(pl.multiple_of(slot * part, 16), part)
        unit(
            lambda g: q_buf[g * many : (g + 1) * many, at, :].reshape(many * part, 128),
            2,
            many * part,
            lambda a, b: kv[u, a:b, :128],
            lambda a, b: kv[u, a:b, 128:],
            jnp.minimum(lens[u], bounds_ref[frame] - block * rows),
            rows,
            acc_ref.at[slot],
            l_ref.at[slot],
            m_ref.at[slot],
            c2,
        )
        return carry

    lax.fori_loop(0, slots * NX, body, 0)
    lane = lax.broadcasted_iota(jnp.int32, (part, 128), 1)
    fill = jnp.zeros((128 - part, 128), jnp.float32)
    under = slots * part
    empty = jnp.zeros((16 - 5 * slots, 128), jnp.float32)
    for g in range(NZ):
        here = slice(g * part, (g + 1) * part)
        table = jnp.zeros((part, 128), jnp.float32)
        for slot in range(slots):
            out[g, slot * part : (slot + 1) * part, :] = acc_ref[slot, here, :].astype(jnp.bfloat16)
            table = jnp.where(lane == slot, m_ref[slot, here, :], table)
            table = jnp.where(lane == slots + slot, l_ref[slot, here, :], table)
        flat = jnp.concatenate([table, fill], axis=0).T
        pieces = three_parts(flat[:slots, :]) + three_parts(flat[slots : 2 * slots, :])[:2]
        flat = jnp.concatenate(pieces + [empty], axis=0)
        out[g, under : under + 16, :] = flat.astype(jnp.bfloat16)


def attn(bounds, queries, kvs, part, c2):
    rows = kvs[0].shape[0] - 16
    slots = NX - 1 if len(kvs) == NX else 2
    anys = pl.BlockSpec(memory_space=pl.ANY)
    return pl.pallas_call(
        functools.partial(attn_kernel, slots, part, rows, c2),
        out_shape=jax.ShapeDtypeStruct((NZ, slots * part + 16, 128), jnp.bfloat16),
        in_specs=[smem, anys] + [anys] * len(kvs),
        out_specs=vmem,
        scratch_shapes=[
            pltpu.VMEM((NZ, slots * part, 128), jnp.bfloat16),
            pltpu.VMEM((len(kvs), -(-rows // 128) * 128, 256), jnp.bfloat16),
            pltpu.VMEM((len(kvs), 16, 256), jnp.bfloat16),
            pltpu.SMEM((len(kvs),), jnp.int32),
        ]
        + [pltpu.VMEM((slots, NZ * part, 128), jnp.float32)] * 3
        + [pltpu.SemaphoreType.DMA] + [pltpu.SemaphoreType.DMA((len(kvs),))] * 2,
        compiler_params=pltpu.CompilerParams(vmem_limit_bytes=VMEM),
        cost_estimate=cost(0.1 if slots == NX - 1 else 16, 1 << 10),
        name="attn",
    )(bounds, queries, *kvs)


def merge_z(ref, part, slots, slot):
    under = slice(slots * part, slots * part + 16)
    tops, totals = [], []
    for s in range(NZ):
        rows16 = ref[s, under, :].astype(jnp.float32)
        pieces = [rows16[k * slots + slot : k * slots + slot + 1, :] for k in range(5)]
        tops.append(pieces[0] + pieces[1] + pieces[2])
        totals.append(pieces[3] + pieces[4])
    top = functools.reduce(jnp.maximum, tops)
    raw = [jnp.exp2(t - top) for t in tops]
    total = functools.reduce(jnp.add, [r * t for r, t in zip(raw, totals)])
    total = jnp.maximum(total, 1.0)
    fill = jnp.zeros((128 - NZ, 128), jnp.float32)
    table = jnp.concatenate([r / total for r in raw] + [fill], axis=0).T
    out = jnp.zeros((part, 128), jnp.float32)
    for s in range(NZ):
        data = ref[s, slot * part : (slot + 1) * part, :].astype(jnp.float32)
        out += table[:part, s : s + 1] * data
    return out.astype(jnp.bfloat16)


def merge_kernel(part, ref, *outs):
    for slot, out in enumerate(outs):
        out[...] = merge_z(ref, part, len(outs), slot)


def merge(payload, part):
    return pl.pallas_call(
        functools.partial(merge_kernel, part),
        out_shape=[jax.ShapeDtypeStruct((part, 128), jnp.bfloat16)] * (NX - 1),
        cost_estimate=cost(2, 1 << 20),
        name="merge",
    )(payload)


def finish_kernel(part, ref, *refs):
    others, out = refs[: NX - 1], refs[NX - 1]
    x = lax.axis_index("x")
    out[:, pl.ds(pl.multiple_of(x * 128, 128), 128)] = merge_z(ref, part, 2, 0)
    out[:, NX * 128 :] = merge_z(ref, part, 2, 1)
    for k, r in enumerate(others):
        head = lax.rem(x + NX - 1 - k, NX)
        out[:, pl.ds(pl.multiple_of(head * 128, 128), 128)] = r[...]


def finish(payload, others, part):
    return pl.pallas_call(
        functools.partial(finish_kernel, part),
        out_shape=jax.ShapeDtypeStruct((part, (NX + 1) * 128), jnp.bfloat16),
        cost_estimate=cost(2, 1 << 20),
        name="finish",
    )(payload, *others)


def exchange(value, axis):
    return lax.all_to_all(value, axis, 0, 0)


def along_x(value, dx):
    return lax.ppermute(value, "x", [(x, (x + dx) % NX) for x in range(NX)])


def attention_part(queries, keys, values, length, bounds, conv):
    part = queries.shape[0]
    c2 = HEAD_DIM ** (-0.5) * LOG2E
    x = lax.axis_index("x")
    packed, last = pack_queries(queries)
    mine = exchange(packed, "x")
    keys, values, _ = lax.optimization_barrier((keys, values, packed))
    cache = pack_cache(length, keys, values)
    kvs = [cache[0]] + [along_x(cache[d], d) for d in range(1, NX)]
    order = lax.dynamic_slice_in_dim(jnp.concatenate([mine, mine]), x + 1, NX, 0)
    order = jnp.concatenate([order.reshape(NX * part, 128), last], axis=0)
    order, _ = lax.optimization_barrier((order, cache[0]))
    everyone = exchange(jnp.broadcast_to(order[None], (NZ,) + order.shape), "z")
    lasts = [cache[NX]] + [along_x(cache[NX], d) for d in range(1, NX)]
    kvs, terms, everyone = lax.optimization_barrier((kvs, conv(cache[0]), everyone))

    landed = exchange(attn(bounds, everyone, kvs, part, c2), "z")
    landed_own = exchange(attn(bounds, everyone, kvs + lasts, part, c2), "z")
    others = [along_x(r, i + 1) for i, r in enumerate(merge(landed, part))]
    return finish(landed_own, others, part), terms


def once(fun, *args):
    shapes = jax.eval_shape(fun, *args)
    turns = 1 + lax.axis_index("x") // NX

    def body(_, carry):
        return lax.optimization_barrier((carry[0], fun(*carry[0])))

    return lax.fori_loop(0, turns, body, (args, jnp.zeros(shapes.shape, shapes.dtype)))[1]


def conv_terms(low, latent, high, norm_gain, conv_weight):
    channels, _, rows, width = latent.shape
    wide = jnp.concatenate([low, latent, high], axis=2)
    squares = jnp.sum(jnp.square(wide.astype(jnp.float32)), axis=0)
    for bit in (1, 2, 4):
        squares = squares + lax.ppermute(squares, "head", head_swap(bit))
    scaled = (
        wide.astype(jnp.float32)
        * lax.rsqrt(squares / CHANNELS + norm_eps)[None]
        * norm_gain[:, None, None, None]
    )
    act = jax.nn.silu(scaled).astype(jnp.bfloat16)
    padded = jnp.pad(act, ((0, 0), (0, 0), (0, 0), (1, 1)))
    windows = [
        padded[:, a, b : b + rows, e : e + width]
        for a in range(3)
        for b in range(3)
        for e in range(3)
    ]
    patches = jnp.concatenate(windows, axis=0)
    weight = conv_weight.reshape(27 * channels, conv_weight.shape[4])
    terms = jnp.einsum("kyx,ko->oyx", patches, weight, preferred_element_type=jnp.float32)
    return terms.astype(jnp.bfloat16).reshape(-1, rows * width)


def neighbour_rows(latent):
    count = lax.axis_size(HIST)
    forward = [(i, i + 1) for i in range(count - 1)]
    backward = [(b, a) for a, b in forward]
    low = lax.ppermute(latent[:, :, -1:], HIST, forward)
    high = lax.ppermute(latent[:, :, :1], HIST, backward)
    return low, high


def conv_sum(terms, conv_bias, shape):
    terms = terms.reshape(NY, 2, shape[0], -1)
    core = lax.rem(lax.axis_index("head"), 2)
    y = lax.axis_index("head") // 2
    kept = lax.dynamic_index_in_dim(terms, core, 1, keepdims=False)
    given = lax.dynamic_index_in_dim(terms, 1 - core, 1, keepdims=False)
    given = lax.ppermute(given, "head", head_swap(1))
    both = kept.astype(jnp.float32) + given.astype(jnp.float32)
    total = lax.dynamic_index_in_dim(both, y, 0, keepdims=False)
    sent = both.astype(jnp.bfloat16)
    for d in range(1, NY):
        piece = lax.dynamic_index_in_dim(sent, lax.rem(y + d, NY), 0, keepdims=False)
        total = total + lax.ppermute(piece, "head", head_shift(d, 0)).astype(jnp.float32)
    out = (total + conv_bias[:, None]).astype(jnp.bfloat16)
    return out.reshape(shape)


def on_device(
    queries,
    cache_keys,
    cache_values,
    hist_lengths,
    frame_bounds,
    latent,
    norm_gain,
    conv_weight,
    conv_bias,
):
    low, high = neighbour_rows(latent)
    attention, terms = attention_part(
        queries,
        cache_keys,
        cache_values,
        hist_lengths,
        frame_bounds,
        lambda after: once(
            conv_terms,
            low,
            lax.optimization_barrier((latent, after))[0],
            high,
            norm_gain,
            conv_weight,
        ),
    )
    shape = (latent.shape[0], latent.shape[2], latent.shape[3])
    return (attention, conv_sum(terms, conv_bias, shape))


def solution(mesh):
    split = jax.sharding.Mesh(
        mesh.devices.reshape(NX, NZ, mesh.shape["head"]), ("x", "z", "head")
    )
    hist = ("x", "z")
    placed = (
        P(hist, "head"),
        P(hist, "head"),
        P(hist, "head"),
        P(hist),
        P(),
        P("head", None, hist, None),
        P("head"),
        P(None, None, None, "head", None),
        P("head"),
    )
    return jax.shard_map(
        on_device,
        mesh=split,
        in_specs=placed,
        out_specs=(P(hist, "head"), P("head", hist, None)),
        check_vma=False,
    )
```

```python
import functools
import math

import jax
import jax.numpy as jnp
from jax import lax
from jax.experimental import pallas as pl
from jax.experimental.pallas import tpu as pltpu
from jax.sharding import PartitionSpec as P

HEAD_DIM = 128
CHANNELS = 384
NX = 4
NZ = 8
NY = 4

NEG = -1e30
LOG2E = math.log2(math.e)
norm_eps = 1e-06
VMEM = 56 << 20
SIZES = (512, 768, 1024, 1152)

HIST = ("x", "z")

vmem = pl.BlockSpec(memory_space=pltpu.VMEM)
smem = pl.BlockSpec(memory_space=pltpu.SMEM)


def head_shift(dy, flip):
    return [
        (y * 2 + c, ((y + dy) % NY) * 2 + (c ^ flip)) for y in range(NY) for c in range(2)
    ]


def head_swap(bit):
    return [(i, i ^ bit) for i in range(2 * NY)]


def dot(a, b, dims):
    return lax.dot_general(a, b, (dims, ((), ())), preferred_element_type=jnp.float32)


def cost(micros, nbytes):
    return pl.CostEstimate(
        flops=int(micros * 1.1e9), bytes_accessed=nbytes, transcendentals=0
    )


def pack_queries_kernel(q_ref, out, last):
    for i in range(NX):
        out[i] = q_ref[:, i * 128 : (i + 1) * 128]
    last[...] = q_ref[:, NX * 128 :]


def pack_queries(queries):
    rows = queries.shape[0]
    return pl.pallas_call(
        pack_queries_kernel,
        out_shape=[
            jax.ShapeDtypeStruct((NX, rows, 128), jnp.bfloat16),
            jax.ShapeDtypeStruct((rows, 128), jnp.bfloat16),
        ],
        cost_estimate=cost(1, 1 << 18),
        name="pack_q",
    )(queries)


def columns(head):
    return pl.ds(pl.multiple_of(head * 128, 128), 128)


def pack_cache_kernel(len_ref, k_ref, v_ref, *outs):
    x = lax.axis_index("x")
    rows = k_ref.shape[0]
    length = len_ref[0]
    row = lax.broadcasted_iota(jnp.int32, (16, 256), 0)
    tail = jnp.where(row == 0, length // 64, jnp.where(row == 1, lax.rem(length, 64), 0))
    tail = tail.astype(jnp.float32).astype(jnp.bfloat16)
    for d, out in enumerate(outs):
        cols = columns(lax.rem(x + d, NX) if d < NX else NX)
        out[:rows, :128] = k_ref[:, cols]
        out[:rows, 128:] = v_ref[:, cols]
        out[rows:, :] = tail


def pack_cache(lengths, keys, values):
    shape = jax.ShapeDtypeStruct((keys.shape[0] + 16, 256), jnp.bfloat16)
    return pl.pallas_call(
        pack_cache_kernel,
        in_specs=[smem, vmem, vmem],
        out_shape=[shape] * (NX + 1),
        compiler_params=pltpu.CompilerParams(vmem_limit_bytes=VMEM),
        cost_estimate=cost(3, 7 << 20),
        name="pack_kv",
    )(lengths, keys, values)


def unit(q_of, n, group, k_of, v_of, limit, rows, acc_ref, l_ref, m_ref, c2):
    def step(low, count):
        row = lax.broadcasted_iota(jnp.int32, (count - low, 128), 0) + low
        seen = row < limit
        first = jnp.broadcast_to(k_of(0, 16).astype(jnp.float32)[:1, :], (count - low, 128))
        k = jnp.where(seen, k_of(low, count).astype(jnp.float32), first).astype(jnp.bfloat16)
        v = jnp.where(seen, v_of(low, count).astype(jnp.float32), 0.0).astype(jnp.bfloat16)
        one = jnp.where(seen, 1.0, 0.0).astype(jnp.bfloat16)
        v = jnp.concatenate([v, one], axis=1)
        if low:
            k = jnp.concatenate([k_of(0, low), k], axis=0)
            ahead = [v_of(0, low), jnp.ones((low, 128), jnp.bfloat16)]
            v = jnp.concatenate([jnp.concatenate(ahead, axis=1), v], axis=0)

        s = dot(q_of(0), k, ((1,), (1,)))
        for g in range(n):
            later = dot(q_of(g + 1), k, ((1,), (1,))) if g + 1 < n else None
            here = slice(g * group, (g + 1) * group)
            old = m_ref[here, :]
            most = functools.reduce(
                jnp.maximum, [s[:, i : i + 128] for i in range(0, count, 128)]
            )
            new = jnp.maximum(old, jnp.max(most, axis=1, keepdims=True) * c2)
            p = jnp.exp2(s * c2 - jnp.concatenate([new] * (count // 128), axis=1)).astype(jnp.bfloat16)
            r = dot(p, v, ((1,), (0,)))
            a = jnp.exp2(old - new)
            acc_ref[here, :] = acc_ref[here, :] * a + r[:, :128]
            l_ref[here, :] = l_ref[here, :] * a + r[:, 128:]
            m_ref[here, :] = new
            s = later

    low = 0
    for size in SIZES + (-(-rows // 128) * 128,):
        pl.when((limit > low) & (limit <= size))(functools.partial(step, low, size))
        low = size


def three_parts(value):
    high = value.astype(jnp.bfloat16).astype(jnp.float32)
    rest = value - high
    mid = rest.astype(jnp.bfloat16).astype(jnp.float32)
    return [high, mid, rest - mid]


def attn_kernel(slots, part, rows, c2, bounds_ref, q_ref, *refs):
    own = slots == 2
    count = 2 * NX if own else NX
    kv_refs, refs = refs[:count], refs[count:]
    out, q_buf, kv, tails, lens, acc_ref, l_ref, m_ref, q_sem, kv_sems, tail_sems = refs
    first = (NX - 1) * part if own else 0
    small = []
    for u, ref in enumerate(kv_refs):
        there = tails.at[u]
        small.append(pltpu.make_async_copy(ref.at[pl.ds(rows, 16), :], there, tail_sems.at[u]))
    for c in small:
        c.start()
    q_copy = pltpu.make_async_copy(q_ref.at[:, pl.ds(first, slots * part), :], q_buf, q_sem)
    q_copy.start()
    for u, ref in enumerate(kv_refs):
        pltpu.make_async_copy(ref, kv.at[u, pl.ds(0, rows + 16), :], kv_sems.at[u]).start()
    acc_ref[...] = jnp.zeros_like(acc_ref)
    l_ref[...] = jnp.zeros_like(l_ref)
    m_ref[...] = jnp.full_like(m_ref, NEG)
    x, z = lax.axis_index("x"), lax.axis_index("z")
    many = NZ // 2

    def kv_copy(u):
        return pltpu.make_async_copy(kv_refs[0], kv.at[u, pl.ds(0, rows + 16), :], kv_sems.at[u])

    row = lax.broadcasted_iota(jnp.int32, (16, 128), 0)
    for u, c in enumerate(small):
        c.wait()
        tail = tails[u, :, :128].astype(jnp.float32)
        high = jnp.max(jnp.where(row == 0, tail, 0.0))
        low = jnp.max(jnp.where(row == 1, tail, 0.0))
        lens[u] = (high * 64.0 + low).astype(jnp.int32)
    q_copy.wait()

    def body(step, carry):
        if own:
            u, slot, frame = step, step // NX, x
            kv_copy(u).wait()
        else:
            u, slot = step // slots, lax.rem(step, slots)
            frame = lax.rem(x + 1 + slot, NX)
            pl.when(slot == 0)(lambda: kv_copy(u).wait())
        block = lax.rem(x + NX - lax.rem(u, NX), NX) * NZ + z
        at = pl.ds(pl.multiple_of(slot * part, 16), part)
        unit(
            lambda g: q_buf[g * many : (g + 1) * many, at, :].reshape(many * part, 128),
            2,
            many * part,
            lambda a, b: kv[u, a:b, :128],
            lambda a, b: kv[u, a:b, 128:],
            jnp.minimum(lens[u], bounds_ref[frame] - block * rows),
            rows,
            acc_ref.at[slot],
            l_ref.at[slot],
            m_ref.at[slot],
            c2,
        )
        return carry

    lax.fori_loop(0, slots * NX, body, 0)
    lane = lax.broadcasted_iota(jnp.int32, (part, 128), 1)
    fill = jnp.zeros((128 - part, 128), jnp.float32)
    under = slots * part
    empty = jnp.zeros((16 - 5 * slots, 128), jnp.float32)
    for g in range(NZ):
        here = slice(g * part, (g + 1) * part)
        table = jnp.zeros((part, 128), jnp.float32)
        for slot in range(slots):
            out[g, slot * part : (slot + 1) * part, :] = acc_ref[slot, here, :].astype(jnp.bfloat16)
            table = jnp.where(lane == slot, m_ref[slot, here, :], table)
            table = jnp.where(lane == slots + slot, l_ref[slot, here, :], table)
        flat = jnp.concatenate([table, fill], axis=0).T
        pieces = three_parts(flat[:slots, :]) + three_parts(flat[slots : 2 * slots, :])[:2]
        flat = jnp.concatenate(pieces + [empty], axis=0)
        out[g, under : under + 16, :] = flat.astype(jnp.bfloat16)


def attn(bounds, queries, kvs, part, c2):
    rows = kvs[0].shape[0] - 16
    slots = NX - 1 if len(kvs) == NX else 2
    anys = pl.BlockSpec(memory_space=pl.ANY)
    return pl.pallas_call(
        functools.partial(attn_kernel, slots, part, rows, c2),
        out_shape=jax.ShapeDtypeStruct((NZ, slots * part + 16, 128), jnp.bfloat16),
        in_specs=[smem, anys] + [anys] * len(kvs),
        out_specs=vmem,
        scratch_shapes=[
            pltpu.VMEM((NZ, slots * part, 128), jnp.bfloat16),
            pltpu.VMEM((len(kvs), -(-rows // 128) * 128, 256), jnp.bfloat16),
            pltpu.VMEM((len(kvs), 16, 256), jnp.bfloat16),
            pltpu.SMEM((len(kvs),), jnp.int32),
        ]
        + [pltpu.VMEM((slots, NZ * part, 128), jnp.float32)] * 3
        + [pltpu.SemaphoreType.DMA] + [pltpu.SemaphoreType.DMA((len(kvs),))] * 2,
        compiler_params=pltpu.CompilerParams(vmem_limit_bytes=VMEM),
        cost_estimate=cost(0.1 if slots == NX - 1 else 16, 1 << 10),
        name="attn",
    )(bounds, queries, *kvs)


def merge_z(ref, part, slots, slot):
    under = slice(slots * part, slots * part + 16)
    tops, totals = [], []
    for s in range(NZ):
        rows16 = ref[s, under, :].astype(jnp.float32)
        pieces = [rows16[k * slots + slot : k * slots + slot + 1, :] for k in range(5)]
        tops.append(pieces[0] + pieces[1] + pieces[2])
        totals.append(pieces[3] + pieces[4])
    top = functools.reduce(jnp.maximum, tops)
    raw = [jnp.exp2(t - top) for t in tops]
    total = functools.reduce(jnp.add, [r * t for r, t in zip(raw, totals)])
    total = jnp.maximum(total, 1.0)
    fill = jnp.zeros((128 - NZ, 128), jnp.float32)
    table = jnp.concatenate([r / total for r in raw] + [fill], axis=0).T
    out = jnp.zeros((part, 128), jnp.float32)
    for s in range(NZ):
        data = ref[s, slot * part : (slot + 1) * part, :].astype(jnp.float32)
        out += table[:part, s : s + 1] * data
    return out.astype(jnp.bfloat16)


def merge_kernel(part, ref, *outs):
    for slot, out in enumerate(outs):
        out[...] = merge_z(ref, part, len(outs), slot)


def merge(payload, part):
    return pl.pallas_call(
        functools.partial(merge_kernel, part),
        out_shape=[jax.ShapeDtypeStruct((part, 128), jnp.bfloat16)] * (NX - 1),
        cost_estimate=cost(2, 1 << 20),
        name="merge",
    )(payload)


def finish_kernel(part, ref, *refs):
    others, out = refs[: NX - 1], refs[NX - 1]
    x = lax.axis_index("x")
    out[:, pl.ds(pl.multiple_of(x * 128, 128), 128)] = merge_z(ref, part, 2, 0)
    out[:, NX * 128 :] = merge_z(ref, part, 2, 1)
    for k, r in enumerate(others):
        head = lax.rem(x + NX - 1 - k, NX)
        out[:, pl.ds(pl.multiple_of(head * 128, 128), 128)] = r[...]


def finish(payload, others, part):
    return pl.pallas_call(
        functools.partial(finish_kernel, part),
        out_shape=jax.ShapeDtypeStruct((part, (NX + 1) * 128), jnp.bfloat16),
        cost_estimate=cost(2, 1 << 20),
        name="finish",
    )(payload, *others)


def exchange(value, axis):
    return lax.all_to_all(value, axis, 0, 0)


def along_x(value, dx):
    return lax.ppermute(value, "x", [(x, (x + dx) % NX) for x in range(NX)])


def attention_part(queries, keys, values, length, bounds, conv):
    part = queries.shape[0]
    c2 = HEAD_DIM ** (-0.5) * LOG2E
    x = lax.axis_index("x")
    packed, last = pack_queries(queries)
    mine = exchange(packed, "x")
    keys, values, _ = lax.optimization_barrier((keys, values, packed))
    cache = pack_cache(length, keys, values)
    kvs = [cache[0]] + [along_x(cache[d], d) for d in range(1, NX)]
    order = lax.dynamic_slice_in_dim(jnp.concatenate([mine, mine]), x + 1, NX, 0)
    order = jnp.concatenate([order.reshape(NX * part, 128), last], axis=0)
    order, _ = lax.optimization_barrier((order, cache[0]))
    everyone = exchange(jnp.broadcast_to(order[None], (NZ,) + order.shape), "z")
    lasts = [cache[NX]] + [along_x(cache[NX], d) for d in range(1, NX)]
    kvs, terms, everyone = lax.optimization_barrier((kvs, conv(cache[0]), everyone))

    landed = exchange(attn(bounds, everyone, kvs, part, c2), "z")
    landed_own = exchange(attn(bounds, everyone, kvs + lasts, part, c2), "z")
    foreign = merge(landed, part)
    others = [along_x(r, i + 1) for i, r in enumerate(foreign)]
    return finish(landed_own, others, part), terms, foreign


def once(fun, *args):
    shapes = jax.eval_shape(fun, *args)
    turns = 1 + lax.axis_index("x") // NX

    def body(_, carry):
        return lax.optimization_barrier((carry[0], fun(*carry[0])))

    return lax.fori_loop(0, turns, body, (args, jnp.zeros(shapes.shape, shapes.dtype)))[1]


def conv_terms(low, latent, high, norm_gain, conv_weight):
    channels, _, rows, width = latent.shape
    wide = jnp.concatenate([low, latent, high], axis=2)
    squares = jnp.sum(jnp.square(wide.astype(jnp.float32)), axis=0)
    for bit in (1, 2, 4):
        squares = squares + lax.ppermute(squares, "head", head_swap(bit))
    scaled = (
        wide.astype(jnp.float32)
        * lax.rsqrt(squares / CHANNELS + norm_eps)[None]
        * norm_gain[:, None, None, None]
    )
    act = jax.nn.silu(scaled).astype(jnp.bfloat16)
    padded = jnp.pad(act, ((0, 0), (0, 0), (0, 0), (1, 1)))
    windows = [
        padded[:, a, b : b + rows, e : e + width]
        for a in range(3)
        for b in range(3)
        for e in range(3)
    ]
    patches = jnp.concatenate(windows, axis=0)
    weight = conv_weight.reshape(27 * channels, conv_weight.shape[4])
    terms = jnp.einsum("kyx,ko->oyx", patches, weight, preferred_element_type=jnp.float32)
    return terms.astype(jnp.bfloat16).reshape(-1, rows * width)


def neighbour_rows(latent):
    count = lax.axis_size(HIST)
    forward = [(i, i + 1) for i in range(count - 1)]
    backward = [(b, a) for a, b in forward]
    low = lax.ppermute(latent[:, :, -1:], HIST, forward)
    high = lax.ppermute(latent[:, :, :1], HIST, backward)
    return low, high


def conv_sum(terms, conv_bias, shape, after):
    terms = terms.reshape(NY, 2, shape[0], -1)
    core = lax.rem(lax.axis_index("head"), 2)
    y = lax.axis_index("head") // 2
    kept = lax.dynamic_index_in_dim(terms, core, 1, keepdims=False)
    given = lax.dynamic_index_in_dim(terms, 1 - core, 1, keepdims=False)
    given = lax.ppermute(given, "head", head_swap(1))
    both = kept.astype(jnp.float32) + given.astype(jnp.float32)
    total = lax.dynamic_index_in_dim(both, y, 0, keepdims=False)
    sent, _ = lax.optimization_barrier((both.astype(jnp.bfloat16), after))
    for d in range(1, NY):
        piece = lax.dynamic_index_in_dim(sent, lax.rem(y + d, NY), 0, keepdims=False)
        total = total + lax.ppermute(piece, "head", head_shift(d, 0)).astype(jnp.float32)
    out = (total + conv_bias[:, None]).astype(jnp.bfloat16)
    return out.reshape(shape)


def on_device(
    queries,
    cache_keys,
    cache_values,
    hist_lengths,
    frame_bounds,
    latent,
    norm_gain,
    conv_weight,
    conv_bias,
):
    low, high = neighbour_rows(latent)
    attention, terms, foreign = attention_part(
        queries,
        cache_keys,
        cache_values,
        hist_lengths,
        frame_bounds,
        lambda after: once(
            conv_terms,
            low,
            lax.optimization_barrier((latent, after))[0],
            high,
            norm_gain,
            conv_weight,
        ),
    )
    shape = (latent.shape[0], latent.shape[2], latent.shape[3])
    return (attention, conv_sum(terms, conv_bias, shape, foreign))


def solution(mesh):
    split = jax.sharding.Mesh(
        mesh.devices.reshape(NX, NZ, mesh.shape["head"]), ("x", "z", "head")
    )
    hist = ("x", "z")
    placed = (
        P(hist, "head"),
        P(hist, "head"),
        P(hist, "head"),
        P(hist),
        P(),
        P("head", None, hist, None),
        P("head"),
        P(None, None, None, "head", None),
        P("head"),
    )
    return jax.shard_map(
        on_device,
        mesh=split,
        in_specs=placed,
        out_specs=(P(hist, "head"), P("head", hist, None)),
        check_vma=False,
    )
```

```python
import functools
import math

import jax
import jax.numpy as jnp
from jax import lax
from jax.experimental import pallas as pl
from jax.experimental.pallas import tpu as pltpu
from jax.sharding import PartitionSpec as P

HEAD_DIM = 128
CHANNELS = 384
NX = 4
NZ = 8
NY = 4

NEG = -1e30
LOG2E = math.log2(math.e)
norm_eps = 1e-06
VMEM = 56 << 20
SIZES = (512, 768, 1024, 1152)

HIST = ("x", "z")

vmem = pl.BlockSpec(memory_space=pltpu.VMEM)
smem = pl.BlockSpec(memory_space=pltpu.SMEM)


def head_shift(dy, flip):
    return [
        (y * 2 + c, ((y + dy) % NY) * 2 + (c ^ flip)) for y in range(NY) for c in range(2)
    ]


def head_swap(bit):
    return [(i, i ^ bit) for i in range(2 * NY)]


def dot(a, b, dims):
    return lax.dot_general(a, b, (dims, ((), ())), preferred_element_type=jnp.float32)


def cost(micros, nbytes):
    return pl.CostEstimate(
        flops=int(micros * 1.1e9), bytes_accessed=nbytes, transcendentals=0
    )


def pack_queries_kernel(q_ref, out, last):
    for i in range(NX):
        out[i] = q_ref[:, i * 128 : (i + 1) * 128]
    last[...] = q_ref[:, NX * 128 :]


def pack_queries(queries):
    rows = queries.shape[0]
    return pl.pallas_call(
        pack_queries_kernel,
        out_shape=[
            jax.ShapeDtypeStruct((NX, rows, 128), jnp.bfloat16),
            jax.ShapeDtypeStruct((rows, 128), jnp.bfloat16),
        ],
        cost_estimate=cost(1, 1 << 18),
        name="pack_q",
    )(queries)


def columns(head):
    return pl.ds(pl.multiple_of(head * 128, 128), 128)


def pack_cache_kernel(len_ref, k_ref, v_ref, *outs):
    x = lax.axis_index("x")
    rows = k_ref.shape[0]
    length = len_ref[0]
    row = lax.broadcasted_iota(jnp.int32, (16, 256), 0)
    tail = jnp.where(row == 0, length // 64, jnp.where(row == 1, lax.rem(length, 64), 0))
    tail = tail.astype(jnp.float32).astype(jnp.bfloat16)
    for d, out in enumerate(outs):
        cols = columns(lax.rem(x + d, NX) if d < NX else NX)
        out[:rows, :128] = k_ref[:, cols]
        out[:rows, 128:] = v_ref[:, cols]
        out[rows:, :] = tail


def pack_cache(lengths, keys, values):
    shape = jax.ShapeDtypeStruct((keys.shape[0] + 16, 256), jnp.bfloat16)
    return pl.pallas_call(
        pack_cache_kernel,
        in_specs=[smem, vmem, vmem],
        out_shape=[shape] * (NX + 1),
        compiler_params=pltpu.CompilerParams(vmem_limit_bytes=VMEM),
        cost_estimate=cost(3, 7 << 20),
        name="pack_kv",
    )(lengths, keys, values)


def unit(q_of, n, group, k_of, v_of, limit, rows, acc_ref, l_ref, m_ref, c2):
    def step(low, count):
        row = lax.broadcasted_iota(jnp.int32, (count - low, 128), 0) + low
        seen = row < limit
        first = jnp.broadcast_to(k_of(0, 16).astype(jnp.float32)[:1, :], (count - low, 128))
        k = jnp.where(seen, k_of(low, count).astype(jnp.float32), first).astype(jnp.bfloat16)
        v = jnp.where(seen, v_of(low, count).astype(jnp.float32), 0.0).astype(jnp.bfloat16)
        one = jnp.where(seen, 1.0, 0.0).astype(jnp.bfloat16)
        v = jnp.concatenate([v, one], axis=1)
        if low:
            k = jnp.concatenate([k_of(0, low), k], axis=0)
            ahead = [v_of(0, low), jnp.ones((low, 128), jnp.bfloat16)]
            v = jnp.concatenate([jnp.concatenate(ahead, axis=1), v], axis=0)

        s = dot(q_of(0), k, ((1,), (1,)))
        for g in range(n):
            later = dot(q_of(g + 1), k, ((1,), (1,))) if g + 1 < n else None
            here = slice(g * group, (g + 1) * group)
            old = m_ref[here, :]
            most = functools.reduce(
                jnp.maximum, [s[:, i : i + 128] for i in range(0, count, 128)]
            )
            new = jnp.maximum(old, jnp.max(most, axis=1, keepdims=True) * c2)
            p = jnp.exp2(s * c2 - jnp.concatenate([new] * (count // 128), axis=1)).astype(jnp.bfloat16)
            r = dot(p, v, ((1,), (0,)))
            a = jnp.exp2(old - new)
            acc_ref[here, :] = acc_ref[here, :] * a + r[:, :128]
            l_ref[here, :] = l_ref[here, :] * a + r[:, 128:]
            m_ref[here, :] = new
            s = later

    low = 0
    for size in SIZES + (-(-rows // 128) * 128,):
        pl.when((limit > low) & (limit <= size))(functools.partial(step, low, size))
        low = size


def three_parts(value):
    high = value.astype(jnp.bfloat16).astype(jnp.float32)
    rest = value - high
    mid = rest.astype(jnp.bfloat16).astype(jnp.float32)
    return [high, mid, rest - mid]


def attn_kernel(slots, part, rows, c2, bounds_ref, q_ref, *refs):
    own = slots == 2
    count = 2 * NX if own else NX
    kv_refs, refs = refs[:count], refs[count:]
    out, q_buf, kv, tails, lens, acc_ref, l_ref, m_ref, q_sem, kv_sems, tail_sems = refs
    first = (NX - 1) * part if own else 0
    small = []
    for u, ref in enumerate(kv_refs):
        there = tails.at[u]
        small.append(pltpu.make_async_copy(ref.at[pl.ds(rows, 16), :], there, tail_sems.at[u]))
    for c in small:
        c.start()
    q_copy = pltpu.make_async_copy(q_ref.at[:, pl.ds(first, slots * part), :], q_buf, q_sem)
    q_copy.start()
    for u, ref in enumerate(kv_refs):
        pltpu.make_async_copy(ref, kv.at[u, pl.ds(0, rows + 16), :], kv_sems.at[u]).start()
    acc_ref[...] = jnp.zeros_like(acc_ref)
    l_ref[...] = jnp.zeros_like(l_ref)
    m_ref[...] = jnp.full_like(m_ref, NEG)
    x, z = lax.axis_index("x"), lax.axis_index("z")
    many = NZ // 2

    def kv_copy(u):
        return pltpu.make_async_copy(kv_refs[0], kv.at[u, pl.ds(0, rows + 16), :], kv_sems.at[u])

    row = lax.broadcasted_iota(jnp.int32, (16, 128), 0)
    for u, c in enumerate(small):
        c.wait()
        tail = tails[u, :, :128].astype(jnp.float32)
        high = jnp.max(jnp.where(row == 0, tail, 0.0))
        low = jnp.max(jnp.where(row == 1, tail, 0.0))
        lens[u] = (high * 64.0 + low).astype(jnp.int32)
    q_copy.wait()

    def body(step, carry):
        if own:
            u, slot, frame = step, step // NX, x
            kv_copy(u).wait()
        else:
            u, slot = step // slots, lax.rem(step, slots)
            frame = lax.rem(x + 1 + slot, NX)
            pl.when(slot == 0)(lambda: kv_copy(u).wait())
        block = lax.rem(x + NX - lax.rem(u, NX), NX) * NZ + z
        at = pl.ds(pl.multiple_of(slot * part, 16), part)
        unit(
            lambda g: q_buf[g * many : (g + 1) * many, at, :].reshape(many * part, 128),
            2,
            many * part,
            lambda a, b: kv[u, a:b, :128],
            lambda a, b: kv[u, a:b, 128:],
            jnp.minimum(lens[u], bounds_ref[frame] - block * rows),
            rows,
            acc_ref.at[slot],
            l_ref.at[slot],
            m_ref.at[slot],
            c2,
        )
        return carry

    lax.fori_loop(0, slots * NX, body, 0)
    lane = lax.broadcasted_iota(jnp.int32, (part, 128), 1)
    fill = jnp.zeros((128 - part, 128), jnp.float32)
    under = slots * part
    empty = jnp.zeros((16 - 5 * slots, 128), jnp.float32)
    for g in range(NZ):
        here = slice(g * part, (g + 1) * part)
        table = jnp.zeros((part, 128), jnp.float32)
        for slot in range(slots):
            out[g, slot * part : (slot + 1) * part, :] = acc_ref[slot, here, :].astype(jnp.bfloat16)
            table = jnp.where(lane == slot, m_ref[slot, here, :], table)
            table = jnp.where(lane == slots + slot, l_ref[slot, here, :], table)
        flat = jnp.concatenate([table, fill], axis=0).T
        pieces = three_parts(flat[:slots, :]) + three_parts(flat[slots : 2 * slots, :])[:2]
        flat = jnp.concatenate(pieces + [empty], axis=0)
        out[g, under : under + 16, :] = flat.astype(jnp.bfloat16)


def attn(bounds, queries, kvs, part, c2):
    rows = kvs[0].shape[0] - 16
    slots = NX - 1 if len(kvs) == NX else 2
    anys = pl.BlockSpec(memory_space=pl.ANY)
    return pl.pallas_call(
        functools.partial(attn_kernel, slots, part, rows, c2),
        out_shape=jax.ShapeDtypeStruct((NZ, slots * part + 16, 128), jnp.bfloat16),
        in_specs=[smem, anys] + [anys] * len(kvs),
        out_specs=vmem,
        scratch_shapes=[
            pltpu.VMEM((NZ, slots * part, 128), jnp.bfloat16),
            pltpu.VMEM((len(kvs), -(-rows // 128) * 128, 256), jnp.bfloat16),
            pltpu.VMEM((len(kvs), 16, 256), jnp.bfloat16),
            pltpu.SMEM((len(kvs),), jnp.int32),
        ]
        + [pltpu.VMEM((slots, NZ * part, 128), jnp.float32)] * 3
        + [pltpu.SemaphoreType.DMA] + [pltpu.SemaphoreType.DMA((len(kvs),))] * 2,
        compiler_params=pltpu.CompilerParams(vmem_limit_bytes=VMEM),
        cost_estimate=cost(0.1 if slots == NX - 1 else 16, 1 << 10),
        name="attn",
    )(bounds, queries, *kvs)


def merge_z(ref, part, slots, slot):
    under = slice(slots * part, slots * part + 16)
    tops, totals = [], []
    for s in range(NZ):
        rows16 = ref[s, under, :].astype(jnp.float32)
        pieces = [rows16[k * slots + slot : k * slots + slot + 1, :] for k in range(5)]
        tops.append(pieces[0] + pieces[1] + pieces[2])
        totals.append(pieces[3] + pieces[4])
    top = functools.reduce(jnp.maximum, tops)
    raw = [jnp.exp2(t - top) for t in tops]
    total = functools.reduce(jnp.add, [r * t for r, t in zip(raw, totals)])
    total = jnp.maximum(total, 1.0)
    fill = jnp.zeros((128 - NZ, 128), jnp.float32)
    table = jnp.concatenate([r / total for r in raw] + [fill], axis=0).T
    out = jnp.zeros((part, 128), jnp.float32)
    for s in range(NZ):
        data = ref[s, slot * part : (slot + 1) * part, :].astype(jnp.float32)
        out += table[:part, s : s + 1] * data
    return out.astype(jnp.bfloat16)


def merge_kernel(part, ref, *outs):
    for slot, out in enumerate(outs):
        out[...] = merge_z(ref, part, len(outs), slot)


def merge(payload, part):
    return pl.pallas_call(
        functools.partial(merge_kernel, part),
        out_shape=[jax.ShapeDtypeStruct((part, 128), jnp.bfloat16)] * (NX - 1),
        cost_estimate=cost(2, 1 << 20),
        name="merge",
    )(payload)


def finish_kernel(part, ref, *refs):
    others, out = refs[: NX - 1], refs[NX - 1]
    x = lax.axis_index("x")
    out[:, pl.ds(pl.multiple_of(x * 128, 128), 128)] = merge_z(ref, part, 2, 0)
    out[:, NX * 128 :] = merge_z(ref, part, 2, 1)
    for k, r in enumerate(others):
        head = lax.rem(x + NX - 1 - k, NX)
        out[:, pl.ds(pl.multiple_of(head * 128, 128), 128)] = r[...]


def finish(payload, others, part):
    return pl.pallas_call(
        functools.partial(finish_kernel, part),
        out_shape=jax.ShapeDtypeStruct((part, (NX + 1) * 128), jnp.bfloat16),
        cost_estimate=cost(2, 1 << 20),
        name="finish",
    )(payload, *others)


def exchange(value, axis):
    return lax.all_to_all(value, axis, 0, 0)


def along_x(value, dx):
    return lax.ppermute(value, "x", [(x, (x + dx) % NX) for x in range(NX)])


def attention_part(queries, keys, values, length, bounds, conv):
    part = queries.shape[0]
    c2 = HEAD_DIM ** (-0.5) * LOG2E
    x = lax.axis_index("x")
    packed, last = pack_queries(queries)
    mine = exchange(packed, "x")
    keys, values, _ = lax.optimization_barrier((keys, values, packed))
    cache = pack_cache(length, keys, values)
    kvs = [cache[0]] + [along_x(cache[d], d) for d in range(1, NX)]
    order = lax.dynamic_slice_in_dim(jnp.concatenate([mine, mine]), x + 1, NX, 0)
    order = jnp.concatenate([order.reshape(NX * part, 128), last], axis=0)
    order, _ = lax.optimization_barrier((order, cache[0]))
    everyone = exchange(jnp.broadcast_to(order[None], (NZ,) + order.shape), "z")
    lasts = [cache[NX]] + [along_x(cache[NX], d) for d in range(1, NX)]
    kvs, terms, everyone = lax.optimization_barrier((kvs, conv(packed, cache[0]), everyone))

    payload = attn(bounds, everyone, kvs, part, c2)
    payload, terms = lax.optimization_barrier((payload, terms))
    landed = exchange(payload, "z")
    landed_own = exchange(attn(bounds, everyone, kvs + lasts, part, c2), "z")
    foreign = merge(landed, part)
    others = [along_x(r, i + 1) for i, r in enumerate(foreign)]
    return finish(landed_own, others, part), terms, foreign


def once(fun, *args):
    shapes = jax.eval_shape(fun, *args)
    turns = 1 + lax.axis_index("x") // NX

    def body(_, carry):
        return lax.optimization_barrier((carry[0], fun(*carry[0])))

    return lax.fori_loop(0, turns, body, (args, jnp.zeros(shapes.shape, shapes.dtype)))[1]


def conv_terms(low, latent, high, norm_gain, conv_weight):
    channels, _, rows, width = latent.shape
    wide = jnp.concatenate([low, latent, high], axis=2)
    squares = jnp.sum(jnp.square(wide.astype(jnp.float32)), axis=0)
    for bit in (1, 2, 4):
        squares = squares + lax.ppermute(squares, "head", head_swap(bit))
    scaled = (
        wide.astype(jnp.float32)
        * lax.rsqrt(squares / CHANNELS + norm_eps)[None]
        * norm_gain[:, None, None, None]
    )
    act = jax.nn.silu(scaled).astype(jnp.bfloat16)
    padded = jnp.pad(act, ((0, 0), (0, 0), (0, 0), (1, 1)))
    windows = [
        padded[:, a, b : b + rows, e : e + width]
        for a in range(3)
        for b in range(3)
        for e in range(3)
    ]
    patches = jnp.concatenate(windows, axis=0)
    weight = conv_weight.reshape(27 * channels, conv_weight.shape[4])
    terms = jnp.einsum("kyx,ko->oyx", patches, weight, preferred_element_type=jnp.float32)
    return terms.astype(jnp.bfloat16).reshape(-1, rows * width)


def conv_after(packed, cache, latent, norm_gain, conv_weight):
    latent, _ = lax.optimization_barrier((latent, packed))
    low, high = neighbour_rows(latent)
    latent, _ = lax.optimization_barrier((latent, cache))
    return once(conv_terms, low, latent, high, norm_gain, conv_weight)


def neighbour_rows(latent):
    count = lax.axis_size(HIST)
    forward = [(i, i + 1) for i in range(count - 1)]
    backward = [(b, a) for a, b in forward]
    low = lax.ppermute(latent[:, :, -1:], HIST, forward)
    high = lax.ppermute(latent[:, :, :1], HIST, backward)
    return low, high


def conv_sum(terms, conv_bias, shape, after):
    terms = terms.reshape(NY, 2, shape[0], -1)
    core = lax.rem(lax.axis_index("head"), 2)
    y = lax.axis_index("head") // 2
    kept = lax.dynamic_index_in_dim(terms, core, 1, keepdims=False)
    given = lax.dynamic_index_in_dim(terms, 1 - core, 1, keepdims=False)
    given = lax.ppermute(given, "head", head_swap(1))
    both = kept.astype(jnp.float32) + given.astype(jnp.float32)
    total = lax.dynamic_index_in_dim(both, y, 0, keepdims=False)
    sent, _ = lax.optimization_barrier((both.astype(jnp.bfloat16), after))
    for d in range(1, NY):
        piece = lax.dynamic_index_in_dim(sent, lax.rem(y + d, NY), 0, keepdims=False)
        total = total + lax.ppermute(piece, "head", head_shift(d, 0)).astype(jnp.float32)
    out = (total + conv_bias[:, None]).astype(jnp.bfloat16)
    return out.reshape(shape)


def on_device(
    queries,
    cache_keys,
    cache_values,
    hist_lengths,
    frame_bounds,
    latent,
    norm_gain,
    conv_weight,
    conv_bias,
):
    attention, terms, foreign = attention_part(
        queries,
        cache_keys,
        cache_values,
        hist_lengths,
        frame_bounds,
        lambda packed, cache: conv_after(packed, cache, latent, norm_gain, conv_weight),
    )
    shape = (latent.shape[0], latent.shape[2], latent.shape[3])
    return (attention, conv_sum(terms, conv_bias, shape, foreign))


def solution(mesh):
    split = jax.sharding.Mesh(
        mesh.devices.reshape(NX, NZ, mesh.shape["head"]), ("x", "z", "head")
    )
    hist = ("x", "z")
    placed = (
        P(hist, "head"),
        P(hist, "head"),
        P(hist, "head"),
        P(hist),
        P(),
        P("head", None, hist, None),
        P("head"),
        P(None, None, None, "head", None),
        P("head"),
    )
    return jax.shard_map(
        on_device,
        mesh=split,
        in_specs=placed,
        out_specs=(P(hist, "head"), P("head", hist, None)),
        check_vma=False,
    )
```
